512 devices in a mesh: grp: 4 (over y), seq: 32 (over z_lo, x), dp: 4 (over z_hi, core).
Axes of the slice: x: 4, y: 4, z: 16 (z_hi: 2, z_lo: 8; z = z_hi * 8 + z_lo), core: 2. Of those that a mesh axis runs over, the one named last changes fastest.
Arguments:
- img_qkv: bfloat16 [32, 16, 3, 1536, 128], P(('grp', 'dp'), None, None, 'seq'), may hold values from -6 to 6
- txt_qkv: bfloat16 [32, 16, 3, 512, 128], P(('grp', 'dp'), None, None, 'seq'), may hold values from -6 to 6
- img_cot: bfloat16 [32, 16, 1536, 128], P(('grp', 'dp'), None, 'seq'), may hold values from -6 to 6
- txt_cot: bfloat16 [32, 16, 512, 128], P(('grp', 'dp'), None, 'seq'), may hold values from -6 to 6
- lengths: int32 [32], P(('grp', 'dp')), may hold values from 1 to 512
- norm_gains: float32 [4, 128], replicated, may hold values from 0.25 to 1.75
Outputs:
- img_out: bfloat16 [32, 16, 1536, 128], P(('grp', 'dp'), None, 'seq')
- txt_out: bfloat16 [32, 16, 512, 128], P(('grp', 'dp'), None, 'seq')
- img_grad: bfloat16 [32, 16, 3, 1536, 128], P(('grp', 'dp'), None, None, 'seq')
- txt_grad: bfloat16 [32, 16, 3, 512, 128], P(('grp', 'dp'), None, None, 'seq')
- gain_grad: float32 [4, 128], replicated
The draws below stay inside these ranges and needn't reach their ends.
All inputs are finite; a program needn't handle non-finite values.
Results may differ from the reference program's by a relative error of at most 0.011.
Values may be sent and summed in bfloat16 or wider, within the bound.
No kernel may reach another device: no remote copies, remote signals or barrier semaphores. Data moves between devices by JAX's collectives and lax.ppermute only.
A program may use at most 64 MiB of HBM per device.

```python
import jax
import jax.numpy as jnp
from jax import lax

HEADS = 16
HD = 128
IMG = 1536
TXT = 512
SAMPLES = 32


def place_ends(drawn, rng, low, high):
    longest = drawn.shape.index(max(drawn.shape))
    spots = []
    for shift in (0, 1):
        where = [jax.random.randint(jax.random.fold_in(rng, axis), (), 0, length) for axis, length in enumerate(drawn.shape)]
        where[longest] = (where[longest] + shift) % drawn.shape[longest]
        spots.append(tuple(where))
    return drawn.at[spots[0]].set(low).at[spots[1]].set(high)


def block_scale(stream_key, shape, cuts, least, largest):
    def one(dim, parts):
        draws = jax.random.uniform(jax.random.fold_in(jax.random.fold_in(stream_key, 6), dim), (parts,), jnp.float32, least / len(cuts), largest / len(cuts))
        return jnp.repeat(jnp.exp(draws), shape[dim] // parts).reshape((-1,) + (1,) * (len(shape) - dim - 1))

    level = one(*cuts[0])
    for cut in cuts[1:]:
        level = level * one(*cut)
    return level


def bell_draw(stream_key, shape, width, limit, split=(), kind=jnp.bfloat16):
    loudness = block_scale(stream_key, shape, split, -0.22, 0.18) if split else 1.0
    result = jax.random.normal(stream_key, shape, jnp.float32) * width * loudness
    return jnp.minimum(jnp.maximum(result, -limit), limit).astype(kind)


def setup_inputs(seed: int = 0) -> dict:
    splits = jax.random.split(jax.random.key(seed), 7)
    img_qkv = bell_draw(splits[0], (SAMPLES, HEADS, 3, IMG, HD), 1.0, 6.0, ((0, 16), (3, 32)))
    txt_qkv = bell_draw(splits[1], (SAMPLES, HEADS, 3, TXT, HD), 1.0, 6.0, ((0, 16), (3, 32)))
    img_cot = bell_draw(splits[2], (SAMPLES, HEADS, IMG, HD), 1.0, 6.0, ((0, 16), (2, 32)))
    txt_cot = bell_draw(splits[3], (SAMPLES, HEADS, TXT, HD), 1.0, 6.0, ((0, 16), (2, 32)))
    lengths = place_ends(jax.random.randint(splits[4], (SAMPLES,), 1, TXT + 1), jax.random.fold_in(splits[4], 1), 1, TXT).astype(jnp.int32)
    norm_gains = jnp.clip(1.0 + 0.15 * jax.random.normal(splits[5], (4, HD), jnp.float32), 0.25, 1.75)
    return dict(img_qkv=img_qkv, txt_qkv=txt_qkv, img_cot=img_cot, txt_cot=txt_cot, lengths=lengths, norm_gains=norm_gains)


def rms_forward(raw_rows, gain_rows):
    values = raw_rows.astype(jnp.float32)
    inverse = lax.rsqrt(lax.optimization_barrier(jnp.mean(values * values, axis=-1, keepdims=True)) + 1e-06)
    return (values * inverse * gain_rows).astype(jnp.bfloat16)

def rms_backward(raw_rows, gain_rows, upstream):
    values = raw_rows.astype(jnp.float32)
    inverse = lax.rsqrt(lax.optimization_barrier(jnp.mean(values * values, axis=-1, keepdims=True)) + 1e-06)
    scaled = gain_rows * upstream
    inner = lax.optimization_barrier(jnp.mean(scaled * values, axis=-1, keepdims=True))
    grad_rows = inverse * scaled - values * inverse * inverse * inverse * inner
    return (grad_rows, upstream * values * inverse)

def pair_math(joint_qkv, cotangent, is_text, key_live, norm_gains):
    head_size = joint_qkv.shape[-1]
    scale = 1.0 / jnp.sqrt(jnp.float32(head_size))
    gain_query = jnp.where(is_text[:, None], norm_gains[2], norm_gains[0])
    gain_key = jnp.where(is_text[:, None], norm_gains[3], norm_gains[1])
    query_normed = rms_forward(joint_qkv[0], gain_query)
    key_normed = rms_forward(joint_qkv[1], gain_key)
    values = joint_qkv[2]
    scores = jnp.dot(query_normed, key_normed.T, preferred_element_type=jnp.float32) * scale
    scores = jnp.where(key_live[None, :], scores, -jnp.inf)
    top_score = lax.optimization_barrier(jnp.max(scores, axis=-1, keepdims=True))
    expo = jnp.exp(scores - top_score)
    probs = expo / lax.optimization_barrier(jnp.sum(expo, axis=-1, keepdims=True))
    probs_b = probs.astype(jnp.bfloat16)
    attended = jnp.dot(probs_b, values, preferred_element_type=jnp.float32).astype(jnp.bfloat16)
    dprobs = jnp.dot(cotangent, values.T, preferred_element_type=jnp.float32)
    delta = lax.optimization_barrier(jnp.sum(probs * dprobs, axis=-1, keepdims=True))
    dscores = (probs * (dprobs - delta) * scale).astype(jnp.bfloat16)
    grad_qn = jnp.dot(dscores, key_normed, preferred_element_type=jnp.float32)
    grad_kn = jnp.dot(dscores.T, query_normed, preferred_element_type=jnp.float32)
    grad_value = jnp.dot(probs_b.T, cotangent, preferred_element_type=jnp.float32).astype(jnp.bfloat16)
    grad_query, terms_query = rms_backward(joint_qkv[0], gain_query, grad_qn)
    grad_key, terms_key = rms_backward(joint_qkv[1], gain_key, grad_kn)
    grads = jnp.stack([grad_query.astype(jnp.bfloat16), grad_key.astype(jnp.bfloat16), grad_value], axis=0)
    text_float = is_text.astype(jnp.float32)[:, None]
    image_float = 1.0 - text_float
    gain_terms = jnp.stack([lax.optimization_barrier(jnp.sum(terms_query * image_float, axis=0)), lax.optimization_barrier(jnp.sum(terms_key * image_float, axis=0)), lax.optimization_barrier(jnp.sum(terms_query * text_float, axis=0)), lax.optimization_barrier(jnp.sum(terms_key * text_float, axis=0))], axis=0)
    return (attended, grads, gain_terms)

def reference(img_qkv, txt_qkv, img_cot, txt_cot, lengths, norm_gains):
    position = jnp.arange(IMG + TXT)
    is_text = position >= IMG

    def one_sample(inputs):
        image_part, text_part, image_cot, text_cot, length = inputs
        joint = jnp.concatenate([image_part, text_part], axis=2)
        joint_cot = jnp.concatenate([image_cot, text_cot], axis=1)
        key_live = jnp.logical_or(jnp.logical_not(is_text), position - IMG < length)

        def one_head(head_inputs):
            return pair_math(head_inputs[0], head_inputs[1], is_text, key_live, norm_gains)
        return lax.map(one_head, (joint, joint_cot))
    attended, grads, gain_terms = lax.map(one_sample, (img_qkv, txt_qkv, img_cot, txt_cot, lengths))
    img_out = attended[:, :, :IMG]
    txt_out = attended[:, :, IMG:]
    img_grad = grads[:, :, :, :IMG]
    txt_grad = grads[:, :, :, IMG:]
    gain_grad = lax.optimization_barrier(jnp.sum(gain_terms, axis=(0, 1)))
    return (img_out, txt_out, img_grad, txt_grad, gain_grad)
```

```python
import functools
import math

import jax
import jax.numpy as jnp
from jax import lax
from jax.experimental import pallas as pl
from jax.experimental.pallas import tpu as pltpu
from jax.sharding import PartitionSpec as P

F32 = jnp.float32
BF16 = jnp.bfloat16
EPS = 1e-06
GROUP = 4
KEY_TILE = 512


def inverse_rms(values):
    return lax.rsqrt(jnp.mean(values * values, axis=-1, keepdims=True) + EPS)


def norm_backward(values, gain, upstream):
    inverse = inverse_rms(values)
    scaled = gain * upstream
    inner = jnp.mean(scaled * values, axis=-1, keepdims=True)
    grad = inverse * scaled - values * (inverse * inverse * inverse * inner)
    return grad, upstream * values * inverse


def pair_kernel(img, txt, length_ref, gains_ref, in_ref, out_ref, terms_ref,
                kn_ref, vaug_ref, eb_ref, dkt_ref, dvt_ref):
    devices = in_ref.shape[0]
    head = in_ref.shape[2]
    blocks = devices // GROUP
    img_block, txt_block = GROUP * img, GROUP * txt
    block = img_block + txt_block
    full = blocks * block
    tile = math.gcd(KEY_TILE, full)
    scale = 1.0 / math.sqrt(head)
    to_exp2 = scale * math.log2(math.e)
    in_txt = 3 * img
    in_cot = 3 * (img + txt)
    out_img = img + txt
    out_txt = out_img + 3 * img
    length = length_ref[0]

    def load(b, img_at, txt_at):
        rows = pl.ds(b * GROUP, GROUP)
        return jnp.concatenate(
            [
                in_ref[rows, img_at : img_at + img].reshape(img_block, head),
                in_ref[rows, txt_at : txt_at + txt].reshape(txt_block, head),
            ],
            axis=0,
        )

    def store(b, img_at, txt_at, values):
        rows = pl.ds(b * GROUP, GROUP)
        out_ref[rows, img_at : img_at + img] = values[:img_block].reshape(GROUP, img, head)
        out_ref[rows, txt_at : txt_at + txt] = values[img_block:].reshape(GROUP, txt, head)

    def gain_rows(which):
        is_img = lax.broadcasted_iota(jnp.int32, (block, head), 0) < img_block
        return jnp.where(is_img, gains_ref[which : which + 1], gains_ref[which + 2 : which + 3])

    def live_rows(b):
        row = lax.broadcasted_iota(jnp.int32, (block, head), 0)
        return jnp.logical_or(row < img_block, row - img_block + b * txt_block < length)

    def add_terms(which, terms):
        terms_ref[which : which + 1] += jnp.sum(terms[:img_block], axis=0, keepdims=True)
        terms_ref[which + 2 : which + 3] += jnp.sum(terms[img_block:], axis=0, keepdims=True)

    terms_ref[...] = jnp.zeros_like(terms_ref)
    dkt_ref[...] = jnp.zeros_like(dkt_ref)
    dvt_ref[...] = jnp.zeros_like(dvt_ref)

    @pl.loop(0, blocks)
    def _keys(b):
        at = pl.ds(pl.multiple_of(b * block, block), block)
        live = live_rows(b)
        raw = load(b, img, in_txt + txt).astype(F32)
        normed = raw * inverse_rms(raw) * gain_rows(1)
        kn_ref[at, :] = jnp.where(live, normed, 0.0).astype(BF16)
        values = load(b, 2 * img, in_txt + 2 * txt).astype(F32)
        vaug_ref[at, :head] = jnp.where(live, values, 0.0).astype(BF16)
        vaug_ref[at, head:] = jnp.where(live, 1.0, 0.0).astype(BF16)

    by_rows = (((1,), (1,)), ((), ()))

    @pl.loop(0, blocks)
    def _queries(b):
        raw = load(b, 0, in_txt).astype(F32)
        gain = gain_rows(0)
        qn = (raw * inverse_rms(raw) * gain).astype(BF16)
        cot = load(b, in_cot, in_cot + img)
        summed = jnp.zeros((block, 2 * head), F32)
        for start in range(0, full, tile):
            keys = slice(start, start + tile)
            scores = lax.dot_general(qn, kn_ref[keys, :], by_rows, preferred_element_type=F32)
            expo = jnp.exp2(scores * to_exp2).astype(BF16)
            eb_ref[:, keys] = expo
            summed += jnp.dot(expo, vaug_ref[keys, :], preferred_element_type=F32)
        per_total = 1.0 / summed[:, head:]
        out = summed[:, :head] * per_total
        store(b, 0, img, out.astype(BF16))
        cot32 = cot.astype(F32)
        delta = jnp.sum(out * cot32, axis=-1, keepdims=True)
        cot_t = jnp.transpose((cot32 * per_total).astype(BF16))
        qn_t = jnp.transpose((qn.astype(F32) * (per_total * scale)).astype(BF16))
        dq = jnp.zeros((block, head), F32)
        for start in range(0, full, tile):
            keys = slice(start, start + tile)
            expo = eb_ref[:, keys]
            dprobs = lax.dot_general(
                cot, vaug_ref[keys, :head], by_rows, preferred_element_type=F32
            )
            dscores = (expo.astype(F32) * (dprobs - delta)).astype(BF16)
            dq += jnp.dot(dscores, kn_ref[keys, :], preferred_element_type=F32)
            dkt_ref[:, keys] += jnp.dot(qn_t, dscores, preferred_element_type=F32)
            dvt_ref[:, keys] += jnp.dot(cot_t, expo, preferred_element_type=F32)
        grad, terms = norm_backward(raw, gain, dq * (per_total * scale))
        store(b, out_img, out_txt, grad.astype(BF16))
        add_terms(0, terms)

    @pl.loop(0, blocks)
    def _key_grads(b):
        at = pl.ds(pl.multiple_of(b * block, block), block)
        live = live_rows(b)
        raw = load(b, img, in_txt + txt).astype(F32)
        dk = jnp.where(live, jnp.transpose(dkt_ref[:, at]), 0.0)
        grad, terms = norm_backward(raw, gain_rows(1), dk)
        store(b, out_img + img, out_txt + txt, grad.astype(BF16))
        add_terms(1, terms)
        dv = jnp.where(live, jnp.transpose(dvt_ref[:, at]), 0.0)
        store(b, out_img + 2 * img, out_txt + 2 * txt, dv.astype(BF16))


def attend_pair(arrived, length, gains, img, txt):
    devices, rows, head = arrived.shape
    full = devices * (img + txt)
    block = GROUP * (img + txt)
    return pl.pallas_call(
        functools.partial(pair_kernel, img, txt),
        out_shape=(
            jax.ShapeDtypeStruct((devices, rows, head), BF16),
            jax.ShapeDtypeStruct((4, head), F32),
        ),
        in_specs=[
            pl.BlockSpec(memory_space=pltpu.SMEM),
            pl.BlockSpec(memory_space=pltpu.VMEM),
            pl.BlockSpec(memory_space=pltpu.VMEM),
        ],
        out_specs=(
            pl.BlockSpec(memory_space=pltpu.VMEM),
            pl.BlockSpec(memory_space=pltpu.VMEM),
        ),
        scratch_shapes=[
            pltpu.VMEM((full, head), BF16),
            pltpu.VMEM((full, 2 * head), BF16),
            pltpu.VMEM((block, full), BF16),
            pltpu.VMEM((head, full), F32),
            pltpu.VMEM((head, full), F32),
        ],
        compiler_params=pltpu.CompilerParams(vmem_limit_bytes=40 * 1024 * 1024),
        cost_estimate=pl.CostEstimate(
            flops=12 * full * full * head,
            bytes_accessed=4 * devices * rows * head,
            transcendentals=full * full,
        ),
        name="attend_pair",
    )(length, gains, arrived)


def sum_everywhere(term, axes):
    count = math.prod(lax.axis_size(axis) for axis in axes)
    step = 1
    while step < count:
        radix = min(8, count // step)
        parts = [term]
        for other in range(1, radix):
            perm = [(i, i ^ (other * step)) for i in range(count)]
            parts.append(lax.ppermute(term, axes, perm))
        while len(parts) > 1:
            parts = [parts[i] + parts[i + 1] for i in range(0, len(parts), 2)]
        term = parts[0]
        step *= radix
    return term


def per_device(img_qkv, txt_qkv, img_cot, txt_cot, lengths, norm_gains):
    samples, heads, _, img, head = img_qkv.shape
    txt = txt_qkv.shape[3]
    pairs = samples * heads
    devices = lax.axis_size("seq")
    assert pairs == devices
    outgoing = jnp.concatenate(
        [
            img_qkv.reshape(pairs, 3 * img, head),
            txt_qkv.reshape(pairs, 3 * txt, head),
            img_cot.reshape(pairs, img, head),
            txt_cot.reshape(pairs, txt, head),
        ],
        axis=1,
    )
    arrived = lax.all_to_all(outgoing, "seq", split_axis=0, concat_axis=0, tiled=True)
    sample = lax.axis_index("seq") // heads
    length = lax.dynamic_slice_in_dim(lengths, sample, 1, 0)
    results, terms = attend_pair(arrived, length, norm_gains, img, txt)
    back = lax.all_to_all(results, "seq", split_axis=0, concat_axis=0, tiled=True)
    gain_grad = sum_everywhere(terms, ("grp", "seq", "dp"))
    own = img + txt
    img_out = back[:, :img].reshape(samples, heads, img, head)
    txt_out = back[:, img:own].reshape(samples, heads, txt, head)
    img_grad = back[:, own : own + 3 * img].reshape(samples, heads, 3, img, head)
    txt_grad = back[:, own + 3 * img :].reshape(samples, heads, 3, txt, head)
    return (img_out, txt_out, img_grad, txt_grad, gain_grad)


def solution(mesh):
    rows = P(("grp", "dp"), None, "seq", None)
    grads = P(("grp", "dp"), None, None, "seq", None)
    return jax.shard_map(
        per_device,
        mesh=mesh,
        in_specs=(grads, grads, rows, rows, P(("grp", "dp")), P()),
        out_specs=(rows, rows, grads, grads, P()),
        check_vma=False,
    )
```

```python
import functools
import math

import jax
import jax.numpy as jnp
from jax import lax
from jax.experimental import pallas as pl
from jax.experimental.pallas import tpu as pltpu
from jax.sharding import PartitionSpec as P

F32 = jnp.float32
BF16 = jnp.bfloat16
EPS = 1e-06
GROUP = 4
KEY_TILE = 512


def inverse_rms(values):
    return lax.rsqrt(jnp.mean(values * values, axis=-1, keepdims=True) + EPS)


def norm_backward(values, gain, upstream):
    inverse = inverse_rms(values)
    scaled = gain * upstream
    inner = jnp.mean(scaled * values, axis=-1, keepdims=True)
    grad = inverse * scaled - values * (inverse * inverse * inverse * inner)
    return grad, upstream * values * inverse


def pair_kernel(img, txt, length_ref, gains_ref, in_ref, out_ref, terms_ref,
                kn_ref, vaug_ref, eb_ref, dkt_ref, dvt_ref):
    devices = in_ref.shape[0]
    head = in_ref.shape[2]
    blocks = devices // GROUP
    img_block, txt_block = GROUP * img, GROUP * txt
    block = img_block + txt_block
    full = blocks * block
    tile = math.gcd(KEY_TILE, full)
    scale = 1.0 / math.sqrt(head)
    to_exp2 = scale * math.log2(math.e)
    in_txt = 3 * img
    in_cot = 3 * (img + txt)
    out_img = img + txt
    out_txt = out_img + 3 * img
    length = length_ref[0]

    def load(b, img_at, txt_at):
        rows = pl.ds(b * GROUP, GROUP)
        return jnp.concatenate(
            [
                in_ref[rows, img_at : img_at + img].reshape(img_block, head),
                in_ref[rows, txt_at : txt_at + txt].reshape(txt_block, head),
            ],
            axis=0,
        )

    def store(b, img_at, txt_at, values):
        rows = pl.ds(b * GROUP, GROUP)
        out_ref[rows, img_at : img_at + img] = values[:img_block].reshape(GROUP, img, head)
        out_ref[rows, txt_at : txt_at + txt] = values[img_block:].reshape(GROUP, txt, head)

    def gain_rows(which):
        is_img = lax.broadcasted_iota(jnp.int32, (block, head), 0) < img_block
        return jnp.where(is_img, gains_ref[which : which + 1], gains_ref[which + 2 : which + 3])

    def live_rows(b):
        row = lax.broadcasted_iota(jnp.int32, (block, head), 0)
        return jnp.logical_or(row < img_block, row - img_block + b * txt_block < length)

    def add_terms(which, terms):
        terms_ref[which : which + 1] += jnp.sum(terms[:img_block], axis=0, keepdims=True)
        terms_ref[which + 2 : which + 3] += jnp.sum(terms[img_block:], axis=0, keepdims=True)

    terms_ref[...] = jnp.zeros_like(terms_ref)
    dkt_ref[...] = jnp.zeros_like(dkt_ref)
    dvt_ref[...] = jnp.zeros_like(dvt_ref)

    @pl.loop(0, blocks)
    def _keys(b):
        at = pl.ds(pl.multiple_of(b * block, block), block)
        live = live_rows(b)
        raw = load(b, img, in_txt + txt).astype(F32)
        normed = raw * inverse_rms(raw) * gain_rows(1)
        kn_ref[at, :] = jnp.where(live, normed, 0.0).astype(BF16)
        values = load(b, 2 * img, in_txt + 2 * txt).astype(F32)
        vaug_ref[at, :head] = jnp.where(live, values, 0.0).astype(BF16)
        vaug_ref[at, head:] = jnp.where(live, 1.0, 0.0).astype(BF16)

    by_rows = (((1,), (1,)), ((), ()))

    def forward(b, held):
        raw = load(b, 0, in_txt).astype(F32)
        gain = gain_rows(0)
        qn = (raw * inverse_rms(raw) * gain).astype(BF16)
        summed = jnp.zeros((block, 2 * head), F32)
        for start in range(0, full, tile):
            keys = slice(start, start + tile)
            scores = lax.dot_general(qn, kn_ref[keys, :], by_rows, preferred_element_type=F32)
            expo = jnp.exp2(scores * to_exp2).astype(BF16)
            held[:, keys] = expo
            summed += jnp.dot(expo, vaug_ref[keys, :], preferred_element_type=F32)
        return raw, gain, qn, summed

    def backward(b, held, raw, gain, qn, summed):
        cot = load(b, in_cot, in_cot + img)
        per_total = 1.0 / summed[:, head:]
        out = summed[:, :head] * per_total
        store(b, 0, img, out.astype(BF16))
        cot32 = cot.astype(F32)
        delta = jnp.sum(out * cot32, axis=-1, keepdims=True)
        cot_t = jnp.transpose((cot32 * per_total).astype(BF16))
        qn_t = jnp.transpose((qn.astype(F32) * (per_total * scale)).astype(BF16))
        dq = jnp.zeros((block, head), F32)
        for start in range(0, full, tile):
            keys = slice(start, start + tile)
            expo = held[:, keys]
            dprobs = lax.dot_general(
                cot, vaug_ref[keys, :head], by_rows, preferred_element_type=F32
            )
            dscores = (expo.astype(F32) * (dprobs - delta)).astype(BF16)
            dq += jnp.dot(dscores, kn_ref[keys, :], preferred_element_type=F32)
            dkt_ref[:, keys] += jnp.dot(qn_t, dscores, preferred_element_type=F32)
            dvt_ref[:, keys] += jnp.dot(cot_t, expo, preferred_element_type=F32)
        grad, terms = norm_backward(raw, gain, dq * (per_total * scale))
        store(b, out_img, out_txt, grad.astype(BF16))
        add_terms(0, terms)

    @pl.loop(0, blocks, step=2)
    def _queries(b):
        first = forward(b, eb_ref.at[0])
        second = forward(b + 1, eb_ref.at[1])
        backward(b, eb_ref.at[0], *first)
        backward(b + 1, eb_ref.at[1], *second)

    @pl.loop(0, blocks)
    def _key_grads(b):
        at = pl.ds(pl.multiple_of(b * block, block), block)
        live = live_rows(b)
        raw = load(b, img, in_txt + txt).astype(F32)
        dk = jnp.where(live, jnp.transpose(dkt_ref[:, at]), 0.0)
        grad, terms = norm_backward(raw, gain_rows(1), dk)
        store(b, out_img + img, out_txt + txt, grad.astype(BF16))
        add_terms(1, terms)
        dv = jnp.where(live, jnp.transpose(dvt_ref[:, at]), 0.0)
        store(b, out_img + 2 * img, out_txt + 2 * txt, dv.astype(BF16))


def attend_pair(arrived, length, gains, img, txt):
    devices, rows, head = arrived.shape
    full = devices * (img + txt)
    block = GROUP * (img + txt)
    return pl.pallas_call(
        functools.partial(pair_kernel, img, txt),
        out_shape=(
            jax.ShapeDtypeStruct((devices, rows, head), BF16),
            jax.ShapeDtypeStruct((4, head), F32),
        ),
        in_specs=[
            pl.BlockSpec(memory_space=pltpu.SMEM),
            pl.BlockSpec(memory_space=pltpu.VMEM),
            pl.BlockSpec(memory_space=pltpu.VMEM),
        ],
        out_specs=(
            pl.BlockSpec(memory_space=pltpu.VMEM),
            pl.BlockSpec(memory_space=pltpu.VMEM),
        ),
        scratch_shapes=[
            pltpu.VMEM((full, head), BF16),
            pltpu.VMEM((full, 2 * head), BF16),
            pltpu.VMEM((2, block, full), BF16),
            pltpu.VMEM((head, full), F32),
            pltpu.VMEM((head, full), F32),
        ],
        compiler_params=pltpu.CompilerParams(vmem_limit_bytes=40 * 1024 * 1024),
        cost_estimate=pl.CostEstimate(
            flops=12 * full * full * head,
            bytes_accessed=4 * devices * rows * head,
            transcendentals=full * full,
        ),
        name="attend_pair",
    )(length, gains, arrived)


def sum_everywhere(term, axes):
    count = math.prod(lax.axis_size(axis) for axis in axes)
    step = 1
    while step < count:
        term = term + lax.ppermute(term, axes, [(i, i ^ step) for i in range(count)])
        step *= 2
    return term


def per_device(img_qkv, txt_qkv, img_cot, txt_cot, lengths, norm_gains):
    samples, heads, _, img, head = img_qkv.shape
    txt = txt_qkv.shape[3]
    pairs = samples * heads
    devices = lax.axis_size("seq")
    assert pairs == devices
    outgoing = jnp.concatenate(
        [
            img_qkv.reshape(pairs, 3 * img, head),
            txt_qkv.reshape(pairs, 3 * txt, head),
            img_cot.reshape(pairs, img, head),
            txt_cot.reshape(pairs, txt, head),
        ],
        axis=1,
    )
    arrived = lax.all_to_all(outgoing, "seq", split_axis=0, concat_axis=0, tiled=True)
    sample = lax.axis_index("seq") // heads
    length = lax.dynamic_slice_in_dim(lengths, sample, 1, 0)
    results, terms = attend_pair(arrived, length, norm_gains, img, txt)
    back = lax.all_to_all(results, "seq", split_axis=0, concat_axis=0, tiled=True)
    gain_grad = sum_everywhere(terms, ("grp", "seq", "dp"))
    own = img + txt
    img_out = back[:, :img].reshape(samples, heads, img, head)
    txt_out = back[:, img:own].reshape(samples, heads, txt, head)
    img_grad = back[:, own : own + 3 * img].reshape(samples, heads, 3, img, head)
    txt_grad = back[:, own + 3 * img :].reshape(samples, heads, 3, txt, head)
    return (img_out, txt_out, img_grad, txt_grad, gain_grad)


def solution(mesh):
    rows = P(("grp", "dp"), None, "seq", None)
    grads = P(("grp", "dp"), None, None, "seq", None)
    return jax.shard_map(
        per_device,
        mesh=mesh,
        in_specs=(grads, grads, rows, rows, P(("grp", "dp")), P()),
        out_specs=(rows, rows, grads, grads, P()),
        check_vma=False,
    )
```

```python
import functools
import math

import jax
import jax.numpy as jnp
from jax import lax
from jax.experimental import pallas as pl
from jax.experimental.pallas import tpu as pltpu
from jax.sharding import PartitionSpec as P

F32 = jnp.float32
BF16 = jnp.bfloat16
EPS = 1e-06
GROUP = 4
KEY_TILE = 512


def inverse_rms(values):
    return lax.rsqrt(jnp.mean(values * values, axis=-1, keepdims=True) + EPS)


def norm_backward(values, gain, upstream):
    inverse = inverse_rms(values)
    scaled = gain * upstream
    inner = jnp.mean(scaled * values, axis=-1, keepdims=True)
    grad = inverse * scaled - values * (inverse * inverse * inverse * inner)
    return grad, upstream * values * inverse


def pair_kernel(img, txt, length_ref, gains_ref, in_ref, out_ref, terms_ref,
                kn_ref, vaug_ref, eb_ref, dkt_ref, dvt_ref):
    devices = in_ref.shape[0]
    head = in_ref.shape[2]
    blocks = devices // GROUP
    img_block, txt_block = GROUP * img, GROUP * txt
    block = img_block + txt_block
    full = blocks * block
    tile = math.gcd(KEY_TILE, full)
    scale = 1.0 / math.sqrt(head)
    to_exp2 = scale * math.log2(math.e)
    in_txt = 3 * img
    in_cot = 3 * (img + txt)
    out_img = img + txt
    out_txt = out_img + 3 * img
    length = length_ref[0]

    def load(b, img_at, txt_at):
        rows = pl.ds(b * GROUP, GROUP)
        return jnp.concatenate(
            [
                in_ref[rows, img_at : img_at + img].reshape(img_block, head),
                in_ref[rows, txt_at : txt_at + txt].reshape(txt_block, head),
            ],
            axis=0,
        )

    def store(b, img_at, txt_at, values):
        rows = pl.ds(b * GROUP, GROUP)
        out_ref[rows, img_at : img_at + img] = values[:img_block].reshape(GROUP, img, head)
        out_ref[rows, txt_at : txt_at + txt] = values[img_block:].reshape(GROUP, txt, head)

    def gain_rows(which):
        is_img = lax.broadcasted_iota(jnp.int32, (block, head), 0) < img_block
        return jnp.where(is_img, gains_ref[which : which + 1], gains_ref[which + 2 : which + 3])

    def live_rows(b):
        row = lax.broadcasted_iota(jnp.int32, (block, head), 0)
        return jnp.logical_or(row < img_block, row - img_block + b * txt_block < length)

    def add_terms(which, terms):
        terms_ref[which : which + 1] += jnp.sum(terms[:img_block], axis=0, keepdims=True)
        terms_ref[which + 2 : which + 3] += jnp.sum(terms[img_block:], axis=0, keepdims=True)

    terms_ref[...] = jnp.zeros_like(terms_ref)
    dkt_ref[...] = jnp.zeros_like(dkt_ref)
    dvt_ref[...] = jnp.zeros_like(dvt_ref)

    @pl.loop(0, blocks)
    def _keys(b):
        at = pl.ds(pl.multiple_of(b * block, block), block)
        live = live_rows(b)
        raw = load(b, img, in_txt + txt).astype(F32)
        normed = raw * inverse_rms(raw) * gain_rows(1)
        kn_ref[at, :] = jnp.where(live, normed, 0.0).astype(BF16)
        values = load(b, 2 * img, in_txt + 2 * txt).astype(F32)
        vaug_ref[at, :head] = jnp.where(live, values, 0.0).astype(BF16)
        vaug_ref[at, head:] = jnp.where(live, 1.0, 0.0).astype(BF16)

    by_rows = (((1,), (1,)), ((), ()))

    def forward(b, held):
        raw = load(b, 0, in_txt).astype(F32)
        gain = gain_rows(0)
        qn = (raw * inverse_rms(raw) * gain).astype(BF16)
        summed = jnp.zeros((block, 2 * head), F32)
        for start in range(0, full, tile):
            keys = slice(start, start + tile)
            scores = lax.dot_general(qn, kn_ref[keys, :], by_rows, preferred_element_type=F32)
            expo = jnp.exp2(scores * to_exp2).astype(BF16)
            held[:, keys] = expo
            summed += jnp.dot(expo, vaug_ref[keys, :], preferred_element_type=F32)
        return raw, gain, qn, summed

    def backward(b, held, raw, gain, qn, summed):
        cot = load(b, in_cot, in_cot + img)
        per_total = 1.0 / summed[:, head:]
        out = summed[:, :head] * per_total
        store(b, 0, img, out.astype(BF16))
        cot32 = cot.astype(F32)
        delta = jnp.sum(out * cot32, axis=-1, keepdims=True)
        cot_t = jnp.transpose((cot32 * per_total).astype(BF16))
        qn_t = jnp.transpose((qn.astype(F32) * (per_total * scale)).astype(BF16))
        dq = jnp.zeros((block, head), F32)
        for start in range(0, full, tile):
            keys = slice(start, start + tile)
            expo = held[:, keys]
            dprobs = lax.dot_general(
                cot, vaug_ref[keys, :head], by_rows, preferred_element_type=F32
            )
            dscores = (expo.astype(F32) * (dprobs - delta)).astype(BF16)
            dq += jnp.dot(dscores, kn_ref[keys, :], preferred_element_type=F32)
            dkt_ref[:, keys] += jnp.dot(qn_t, dscores, preferred_element_type=F32)
            dvt_ref[:, keys] += jnp.dot(cot_t, expo, preferred_element_type=F32)
        grad, terms = norm_backward(raw, gain, dq * (per_total * scale))
        store(b, out_img, out_txt, grad.astype(BF16))
        add_terms(0, terms)

    @pl.loop(0, blocks, step=2)
    def _queries(b):
        first = forward(b, eb_ref.at[0])
        second = forward(b + 1, eb_ref.at[1])
        backward(b, eb_ref.at[0], *first)
        backward(b + 1, eb_ref.at[1], *second)

    @pl.loop(0, blocks)
    def _key_grads(b):
        at = pl.ds(pl.multiple_of(b * block, block), block)
        live = live_rows(b)
        raw = load(b, img, in_txt + txt).astype(F32)
        dk = jnp.where(live, jnp.transpose(dkt_ref[:, at]), 0.0)
        grad, terms = norm_backward(raw, gain_rows(1), dk)
        store(b, out_img + img, out_txt + txt, grad.astype(BF16))
        add_terms(1, terms)
        dv = jnp.where(live, jnp.transpose(dvt_ref[:, at]), 0.0)
        store(b, out_img + 2 * img, out_txt + 2 * txt, dv.astype(BF16))


def attend_pair(arrived, length, gains, img, txt):
    devices, rows, head = arrived.shape
    full = devices * (img + txt)
    block = GROUP * (img + txt)
    return pl.pallas_call(
        functools.partial(pair_kernel, img, txt),
        out_shape=(
            jax.ShapeDtypeStruct((devices, rows, head), BF16),
            jax.ShapeDtypeStruct((4, head), F32),
        ),
        in_specs=[
            pl.BlockSpec(memory_space=pltpu.SMEM),
            pl.BlockSpec(memory_space=pltpu.VMEM),
            pl.BlockSpec(memory_space=pltpu.VMEM),
        ],
        out_specs=(
            pl.BlockSpec(memory_space=pltpu.VMEM),
            pl.BlockSpec(memory_space=pltpu.VMEM),
        ),
        scratch_shapes=[
            pltpu.VMEM((full, head), BF16),
            pltpu.VMEM((full, 2 * head), BF16),
            pltpu.VMEM((2, block, full), BF16),
            pltpu.VMEM((head, full), F32),
            pltpu.VMEM((head, full), F32),
        ],
        compiler_params=pltpu.CompilerParams(vmem_limit_bytes=40 * 1024 * 1024),
        cost_estimate=pl.CostEstimate(
            flops=12 * full * full * head,
            bytes_accessed=4 * devices * rows * head,
            transcendentals=full * full,
        ),
        name="attend_pair",
    )(length, gains, arrived)


def per_device(img_qkv, txt_qkv, img_cot, txt_cot, lengths, norm_gains):
    samples, heads, _, img, head = img_qkv.shape
    txt = txt_qkv.shape[3]
    pairs = samples * heads
    devices = lax.axis_size("seq")
    assert pairs == devices
    outgoing = jnp.concatenate(
        [
            img_qkv.reshape(pairs, 3 * img, head),
            txt_qkv.reshape(pairs, 3 * txt, head),
            img_cot.reshape(pairs, img, head),
            txt_cot.reshape(pairs, txt, head),
        ],
        axis=1,
    )
    arrived = lax.all_to_all(outgoing, "seq", split_axis=0, concat_axis=0, tiled=True)
    sample = lax.axis_index("seq") // heads
    length = lax.dynamic_slice_in_dim(lengths, sample, 1, 0)
    results, terms = attend_pair(arrived, length, norm_gains, img, txt)
    back = lax.all_to_all(results, "seq", split_axis=0, concat_axis=0, tiled=True)
    gain_grad = jnp.sum(lax.all_gather(terms, ("grp", "seq", "dp")), axis=0)
    own = img + txt
    img_out = back[:, :img].reshape(samples, heads, img, head)
    txt_out = back[:, img:own].reshape(samples, heads, txt, head)
    img_grad = back[:, own : own + 3 * img].reshape(samples, heads, 3, img, head)
    txt_grad = back[:, own + 3 * img :].reshape(samples, heads, 3, txt, head)
    return (img_out, txt_out, img_grad, txt_grad, gain_grad)


def solution(mesh):
    rows = P(("grp", "dp"), None, "seq", None)
    grads = P(("grp", "dp"), None, None, "seq", None)
    return jax.shard_map(
        per_device,
        mesh=mesh,
        in_specs=(grads, grads, rows, rows, P(("grp", "dp")), P()),
        out_specs=(rows, rows, grads, grads, P()),
        check_vma=False,
    )
```

```python
import functools
import math

import jax
import jax.numpy as jnp
from jax import lax
from jax.experimental import pallas as pl
from jax.experimental.pallas import tpu as pltpu
from jax.sharding import PartitionSpec as P

F32 = jnp.float32
BF16 = jnp.bfloat16
EPS = 1e-06
GROUP = 8
KEY_TILE = 512


def inverse_rms(values):
    return lax.rsqrt(jnp.mean(values * values, axis=-1, keepdims=True) + EPS)


def norm_backward(values, gain, upstream):
    inverse = inverse_rms(values)
    scaled = gain * upstream
    inner = jnp.mean(scaled * values, axis=-1, keepdims=True)
    grad = inverse * scaled - values * (inverse * inverse * inverse * inner)
    return grad, upstream * values * inverse


def pair_kernel(img, txt, length_ref, gains_ref, in_ref, out_ref, terms_ref,
                kn_ref, vaug_ref, eb_ref, dkt_ref, dvt_ref):
    devices = in_ref.shape[0]
    head = in_ref.shape[2]
    blocks = devices // GROUP
    img_block, txt_block = GROUP * img, GROUP * txt
    block = img_block + txt_block
    full = blocks * block
    tile = math.gcd(KEY_TILE, full)
    scale = 1.0 / math.sqrt(head)
    to_exp2 = scale * math.log2(math.e)
    in_txt = 3 * img
    in_cot = 3 * (img + txt)
    out_img = img + txt
    out_txt = out_img + 3 * img
    length = length_ref[0]

    def load(b, img_at, txt_at):
        rows = pl.ds(b * GROUP, GROUP)
        return jnp.concatenate(
            [
                in_ref[rows, img_at : img_at + img].reshape(img_block, head),
                in_ref[rows, txt_at : txt_at + txt].reshape(txt_block, head),
            ],
            axis=0,
        )

    def store(b, img_at, txt_at, values):
        rows = pl.ds(b * GROUP, GROUP)
        out_ref[rows, img_at : img_at + img] = values[:img_block].reshape(GROUP, img, head)
        out_ref[rows, txt_at : txt_at + txt] = values[img_block:].reshape(GROUP, txt, head)

    def gain_rows(which):
        is_img = lax.broadcasted_iota(jnp.int32, (block, head), 0) < img_block
        return jnp.where(is_img, gains_ref[which : which + 1], gains_ref[which + 2 : which + 3])

    def live_rows(b):
        row = lax.broadcasted_iota(jnp.int32, (block, head), 0)
        return jnp.logical_or(row < img_block, row - img_block + b * txt_block < length)

    def add_terms(which, terms):
        terms_ref[which : which + 1] += jnp.sum(terms[:img_block], axis=0, keepdims=True)
        terms_ref[which + 2 : which + 3] += jnp.sum(terms[img_block:], axis=0, keepdims=True)

    terms_ref[...] = jnp.zeros_like(terms_ref)
    dkt_ref[...] = jnp.zeros_like(dkt_ref)
    dvt_ref[...] = jnp.zeros_like(dvt_ref)

    for b in range(blocks):
        at = slice(b * block, (b + 1) * block)
        live = live_rows(b)
        raw = load(b, img, in_txt + txt).astype(F32)
        normed = raw * inverse_rms(raw) * gain_rows(1)
        kn_ref[at, :] = jnp.where(live, normed, 0.0).astype(BF16)
        values = load(b, 2 * img, in_txt + 2 * txt).astype(F32)
        vaug_ref[at, :head] = jnp.where(live, values, 0.0).astype(BF16)
        vaug_ref[at, head:] = jnp.where(live, 1.0, 0.0).astype(BF16)

    by_rows = (((1,), (1,)), ((), ()))

    def forward(b, held):
        raw = load(b, 0, in_txt).astype(F32)
        gain = gain_rows(0)
        qn = (raw * inverse_rms(raw) * gain).astype(BF16)
        summed = jnp.zeros((block, 2 * head), F32)
        for start in range(0, full, tile):
            keys = slice(start, start + tile)
            scores = lax.dot_general(qn, kn_ref[keys, :], by_rows, preferred_element_type=F32)
            expo = jnp.exp2(scores * to_exp2).astype(BF16)
            held[:, keys] = expo
            summed += jnp.dot(expo, vaug_ref[keys, :], preferred_element_type=F32)
        return raw, gain, qn, summed

    def backward(b, held, raw, gain, qn, summed):
        cot = load(b, in_cot, in_cot + img)
        per_total = 1.0 / summed[:, head:]
        out = summed[:, :head] * per_total
        store(b, 0, img, out.astype(BF16))
        cot32 = cot.astype(F32)
        delta = jnp.sum(out * cot32, axis=-1, keepdims=True)
        cot_t = jnp.transpose((cot32 * per_total).astype(BF16))
        qn_t = jnp.transpose((qn.astype(F32) * (per_total * scale)).astype(BF16))
        dq = jnp.zeros((block, head), F32)
        for start in range(0, full, tile):
            keys = slice(start, start + tile)
            expo = held[:, keys]
            dprobs = lax.dot_general(
                cot, vaug_ref[keys, :head], by_rows, preferred_element_type=F32
            )
            dscores = expo * (dprobs - delta).astype(BF16)
            dq += jnp.dot(dscores, kn_ref[keys, :], preferred_element_type=F32)
            dkt_ref[:, keys] += jnp.dot(qn_t, dscores, preferred_element_type=F32)
            dvt_ref[:, keys] += jnp.dot(cot_t, expo, preferred_element_type=F32)
        grad, terms = norm_backward(raw, gain, dq * (per_total * scale))
        store(b, out_img, out_txt, grad.astype(BF16))
        add_terms(0, terms)

    @pl.loop(0, blocks, step=2)
    def _queries(b):
        first = forward(b, eb_ref.at[0])
        second = forward(b + 1, eb_ref.at[1])
        backward(b, eb_ref.at[0], *first)
        backward(b + 1, eb_ref.at[1], *second)

    @pl.loop(0, blocks)
    def _key_grads(b):
        at = pl.ds(pl.multiple_of(b * block, block), block)
        live = live_rows(b)
        raw = load(b, img, in_txt + txt).astype(F32)
        dk = jnp.where(live, jnp.transpose(dkt_ref[:, at]), 0.0)
        grad, terms = norm_backward(raw, gain_rows(1), dk)
        store(b, out_img + img, out_txt + txt, grad.astype(BF16))
        add_terms(1, terms)
        dv = jnp.where(live, jnp.transpose(dvt_ref[:, at]), 0.0)
        store(b, out_img + 2 * img, out_txt + 2 * txt, dv.astype(BF16))


def attend_pair(arrived, length, gains, img, txt):
    devices, rows, head = arrived.shape
    full = devices * (img + txt)
    block = GROUP * (img + txt)
    return pl.pallas_call(
        functools.partial(pair_kernel, img, txt),
        out_shape=(
            jax.ShapeDtypeStruct((devices, rows, head), BF16),
            jax.ShapeDtypeStruct((4, head), F32),
        ),
        in_specs=[
            pl.BlockSpec(memory_space=pltpu.SMEM),
            pl.BlockSpec(memory_space=pltpu.VMEM),
            pl.BlockSpec(memory_space=pltpu.VMEM),
        ],
        out_specs=(
            pl.BlockSpec(memory_space=pltpu.VMEM),
            pl.BlockSpec(memory_space=pltpu.VMEM),
        ),
        scratch_shapes=[
            pltpu.VMEM((full, head), BF16),
            pltpu.VMEM((full, 2 * head), BF16),
            pltpu.VMEM((2, block, full), BF16),
            pltpu.VMEM((head, full), F32),
            pltpu.VMEM((head, full), F32),
        ],
        compiler_params=pltpu.CompilerParams(vmem_limit_bytes=40 * 1024 * 1024),
        cost_estimate=pl.CostEstimate(
            flops=12 * full * full * head,
            bytes_accessed=4 * devices * rows * head,
            transcendentals=full * full,
        ),
        name="attend_pair",
    )(length, gains, arrived)


def sum_pairwise(term, axis, steps):
    count = lax.axis_size(axis)
    for step in steps:
        term = term + lax.ppermute(term, axis, [(i, i ^ step) for i in range(count)])
    return term


def powers_of_two(count):
    return [1 << bit for bit in range(count.bit_length() - 1)]


def per_device(img_qkv, txt_qkv, img_cot, txt_cot, lengths, norm_gains):
    samples, heads, _, img, head = img_qkv.shape
    txt = txt_qkv.shape[3]
    pairs = samples * heads
    devices = lax.axis_size("seq")
    assert pairs == devices
    outgoing = jnp.concatenate(
        [
            img_qkv.reshape(pairs, 3 * img, head),
            txt_qkv.reshape(pairs, 3 * txt, head),
            img_cot.reshape(pairs, img, head),
            txt_cot.reshape(pairs, txt, head),
        ],
        axis=1,
    )
    arrived = lax.all_to_all(outgoing, "seq", split_axis=0, concat_axis=0, tiled=True)
    sample = lax.axis_index("seq") // heads
    length = lax.dynamic_slice_in_dim(lengths, sample, 1, 0)
    results, terms = attend_pair(arrived, length, norm_gains, img, txt)
    back = lax.all_to_all(results, "seq", split_axis=0, concat_axis=0, tiled=True)
    for axis in ("grp", "dp"):
        terms = sum_pairwise(terms, axis, powers_of_two(lax.axis_size(axis)))
    back, terms = lax.optimization_barrier((back, terms))
    copies = jnp.broadcast_to(terms[None], (devices,) + terms.shape)
    group_terms = lax.all_to_all(copies, "seq", split_axis=0, concat_axis=0, tiled=True)
    gain_grad = jnp.sum(group_terms, axis=0)
    own = img + txt
    img_out = back[:, :img].reshape(samples, heads, img, head)
    txt_out = back[:, img:own].reshape(samples, heads, txt, head)
    img_grad = back[:, own : own + 3 * img].reshape(samples, heads, 3, img, head)
    txt_grad = back[:, own + 3 * img :].reshape(samples, heads, 3, txt, head)
    return (img_out, txt_out, img_grad, txt_grad, gain_grad)


def solution(mesh):
    rows = P(("grp", "dp"), None, "seq", None)
    grads = P(("grp", "dp"), None, None, "seq", None)
    return jax.shard_map(
        per_device,
        mesh=mesh,
        in_specs=(grads, grads, rows, rows, P(("grp", "dp")), P()),
        out_specs=(rows, rows, grads, grads, P()),
        check_vma=False,
    )
```

```python
import functools
import math

import jax
import jax.numpy as jnp
from jax import lax
from jax.experimental import pallas as pl
from jax.experimental.pallas import tpu as pltpu
from jax.sharding import PartitionSpec as P

F32 = jnp.float32
BF16 = jnp.bfloat16
EPS = 1e-06
GROUP = 8
KEY_TILE = 512
ALONG_X = 4


def inverse_rms(values):
    return lax.rsqrt(jnp.mean(values * values, axis=-1, keepdims=True) + EPS)


def norm_backward(values, gain, upstream):
    inverse = inverse_rms(values)
    scaled = gain * upstream
    inner = jnp.mean(scaled * values, axis=-1, keepdims=True)
    grad = inverse * scaled - values * (inverse * inverse * inverse * inner)
    return grad, upstream * values * inverse


def pair_kernel(img, txt, length_ref, gains_ref, in_ref, out_ref, terms_ref,
                kn_ref, vaug_ref, eb_ref, dkt_ref, dvt_ref):
    devices = in_ref.shape[0]
    head = in_ref.shape[2]
    blocks = devices // GROUP
    img_block, txt_block = GROUP * img, GROUP * txt
    block = img_block + txt_block
    full = blocks * block
    tile = math.gcd(KEY_TILE, full)
    scale = 1.0 / math.sqrt(head)
    to_exp2 = scale * math.log2(math.e)
    in_txt = 3 * img
    in_cot = 3 * (img + txt)
    out_img = img + txt
    out_txt = out_img + 3 * img
    length = length_ref[0]

    def load(b, img_at, txt_at):
        rows = pl.ds(b * GROUP, GROUP)
        return jnp.concatenate(
            [
                in_ref[rows, img_at : img_at + img].reshape(img_block, head),
                in_ref[rows, txt_at : txt_at + txt].reshape(txt_block, head),
            ],
            axis=0,
        )

    def store(b, img_at, txt_at, values):
        rows = pl.ds(b * GROUP, GROUP)
        out_ref[rows, img_at : img_at + img] = values[:img_block].reshape(GROUP, img, head)
        out_ref[rows, txt_at : txt_at + txt] = values[img_block:].reshape(GROUP, txt, head)

    def gain_rows(which):
        is_img = lax.broadcasted_iota(jnp.int32, (block, head), 0) < img_block
        return jnp.where(is_img, gains_ref[which : which + 1], gains_ref[which + 2 : which + 3])

    def live_rows(b):
        row = lax.broadcasted_iota(jnp.int32, (block, head), 0)
        return jnp.logical_or(row < img_block, row - img_block + b * txt_block < length)

    def add_terms(which, terms):
        terms_ref[which : which + 1] += jnp.sum(terms[:img_block], axis=0, keepdims=True)
        terms_ref[which + 2 : which + 3] += jnp.sum(terms[img_block:], axis=0, keepdims=True)

    terms_ref[...] = jnp.zeros_like(terms_ref)
    dkt_ref[...] = jnp.zeros_like(dkt_ref)
    dvt_ref[...] = jnp.zeros_like(dvt_ref)

    for b in range(blocks):
        at = slice(b * block, (b + 1) * block)
        live = live_rows(b)
        raw = load(b, img, in_txt + txt).astype(F32)
        normed = raw * inverse_rms(raw) * gain_rows(1)
        kn_ref[at, :] = jnp.where(live, normed, 0.0).astype(BF16)
        values = load(b, 2 * img, in_txt + 2 * txt).astype(F32)
        vaug_ref[at, :head] = jnp.where(live, values, 0.0).astype(BF16)
        vaug_ref[at, head:] = jnp.where(live, 1.0, 0.0).astype(BF16)

    by_rows = (((1,), (1,)), ((), ()))

    def forward(b, held):
        raw = load(b, 0, in_txt).astype(F32)
        gain = gain_rows(0)
        qn = (raw * inverse_rms(raw) * gain).astype(BF16)
        summed = jnp.zeros((block, 2 * head), F32)
        for start in range(0, full, tile):
            keys = slice(start, start + tile)
            scores = lax.dot_general(qn, kn_ref[keys, :], by_rows, preferred_element_type=F32)
            expo = jnp.exp2(scores * to_exp2).astype(BF16)
            held[:, keys] = expo
            summed += jnp.dot(expo, vaug_ref[keys, :], preferred_element_type=F32)
        return raw, gain, qn, summed

    def backward(b, held, raw, gain, qn, summed):
        cot = load(b, in_cot, in_cot + img)
        per_total = 1.0 / summed[:, head:]
        out = summed[:, :head] * per_total
        store(b, 0, img, out.astype(BF16))
        cot32 = cot.astype(F32)
        delta = jnp.sum(out * cot32, axis=-1, keepdims=True)
        cot_t = jnp.transpose((cot32 * per_total).astype(BF16))
        qn_t = jnp.transpose((qn.astype(F32) * (per_total * scale)).astype(BF16))
        dq = jnp.zeros((block, head), F32)
        for start in range(0, full, tile):
            keys = slice(start, start + tile)
            expo = held[:, keys]
            dprobs = lax.dot_general(
                cot, vaug_ref[keys, :head], by_rows, preferred_element_type=F32
            )
            dscores = expo * (dprobs - delta).astype(BF16)
            dq += jnp.dot(dscores, kn_ref[keys, :], preferred_element_type=F32)
            dkt_ref[:, keys] += jnp.dot(qn_t, dscores, preferred_element_type=F32)
            dvt_ref[:, keys] += jnp.dot(cot_t, expo, preferred_element_type=F32)
        grad, terms = norm_backward(raw, gain, dq * (per_total * scale))
        store(b, out_img, out_txt, grad.astype(BF16))
        add_terms(0, terms)

    @pl.loop(0, blocks, step=2)
    def _queries(b):
        first = forward(b, eb_ref.at[0])
        second = forward(b + 1, eb_ref.at[1])
        backward(b, eb_ref.at[0], *first)
        backward(b + 1, eb_ref.at[1], *second)

    @pl.loop(0, blocks)
    def _key_grads(b):
        at = pl.ds(pl.multiple_of(b * block, block), block)
        live = live_rows(b)
        raw = load(b, img, in_txt + txt).astype(F32)
        dk = jnp.where(live, jnp.transpose(dkt_ref[:, at]), 0.0)
        grad, terms = norm_backward(raw, gain_rows(1), dk)
        store(b, out_img + img, out_txt + txt, grad.astype(BF16))
        add_terms(1, terms)
        dv = jnp.where(live, jnp.transpose(dvt_ref[:, at]), 0.0)
        store(b, out_img + 2 * img, out_txt + 2 * txt, dv.astype(BF16))


def attend_pair(arrived, length, gains, img, txt):
    devices, rows, head = arrived.shape
    full = devices * (img + txt)
    block = GROUP * (img + txt)
    return pl.pallas_call(
        functools.partial(pair_kernel, img, txt),
        out_shape=(
            jax.ShapeDtypeStruct((devices, rows, head), BF16),
            jax.ShapeDtypeStruct((4, head), F32),
        ),
        in_specs=[
            pl.BlockSpec(memory_space=pltpu.SMEM),
            pl.BlockSpec(memory_space=pltpu.VMEM),
            pl.BlockSpec(memory_space=pltpu.VMEM),
        ],
        out_specs=(
            pl.BlockSpec(memory_space=pltpu.VMEM),
            pl.BlockSpec(memory_space=pltpu.VMEM),
        ),
        scratch_shapes=[
            pltpu.VMEM((full, head), BF16),
            pltpu.VMEM((full, 2 * head), BF16),
            pltpu.VMEM((2, block, full), BF16),
            pltpu.VMEM((head, full), F32),
            pltpu.VMEM((head, full), F32),
        ],
        compiler_params=pltpu.CompilerParams(vmem_limit_bytes=40 * 1024 * 1024),
        cost_estimate=pl.CostEstimate(
            flops=12 * full * full * head,
            bytes_accessed=4 * devices * rows * head,
            transcendentals=full * full,
        ),
        name="attend_pair",
    )(length, gains, arrived)


def pack_kernel(*refs):
    *parts, out_ref, sems = refs
    copies = []
    at = 0
    for i, part in enumerate(parts):
        rows = part.shape[1]
        copies.append(pltpu.make_async_copy(part, out_ref.at[:, at : at + rows], sems.at[i]))
        at += rows
    for copy in copies:
        copy.start()
    for copy in copies:
        copy.wait()


def pack_rows(*parts):
    pairs, _, head = parts[0].shape
    rows = sum(part.shape[1] for part in parts)
    return pl.pallas_call(
        pack_kernel,
        out_shape=jax.ShapeDtypeStruct((pairs, rows, head), BF16),
        in_specs=[pl.BlockSpec(memory_space=pl.ANY)] * len(parts),
        out_specs=pl.BlockSpec(memory_space=pl.ANY),
        scratch_shapes=[pltpu.SemaphoreType.DMA((len(parts),))],
        name="pack_rows",
    )(*parts)


def sum_pairwise(term, axis, steps):
    count = lax.axis_size(axis)
    for step in steps:
        term = term + lax.ppermute(term, axis, [(i, i ^ step) for i in range(count)])
    return term


def powers_of_two(count):
    return [1 << bit for bit in range(count.bit_length() - 1)]


def per_device(img_qkv, txt_qkv, img_cot, txt_cot, lengths, norm_gains):
    samples, heads, _, img, head = img_qkv.shape
    txt = txt_qkv.shape[3]
    pairs = samples * heads
    devices = lax.axis_size("seq")
    assert pairs == devices
    outgoing = pack_rows(
        img_qkv.reshape(pairs, 3 * img, head),
        txt_qkv.reshape(pairs, 3 * txt, head),
        img_cot.reshape(pairs, img, head),
        txt_cot.reshape(pairs, txt, head),
    )
    arrived = lax.all_to_all(outgoing, "seq", split_axis=0, concat_axis=0, tiled=True)
    sample = lax.axis_index("seq") // heads
    length = lax.dynamic_slice_in_dim(lengths, sample, 1, 0)
    results, terms = attend_pair(arrived, length, norm_gains, img, txt)
    back = lax.all_to_all(results, "seq", split_axis=0, concat_axis=0, tiled=True)
    for axis in ("grp", "dp"):
        terms = sum_pairwise(terms, axis, powers_of_two(lax.axis_size(axis)))
    terms = sum_pairwise(terms, "seq", powers_of_two(ALONG_X))
    ends = devices // ALONG_X
    copies = jnp.broadcast_to(terms[None], (ends,) + terms.shape)
    back, copies = lax.optimization_barrier((back, copies))
    lines = [[x + ALONG_X * z for z in range(ends)] for x in range(ALONG_X)]
    line_terms = lax.all_to_all(
        copies, "seq", split_axis=0, concat_axis=0, axis_index_groups=lines, tiled=True
    )
    gain_grad = jnp.sum(line_terms, axis=0)
    own = img + txt
    img_out = back[:, :img].reshape(samples, heads, img, head)
    txt_out = back[:, img:own].reshape(samples, heads, txt, head)
    img_grad = back[:, own : own + 3 * img].reshape(samples, heads, 3, img, head)
    txt_grad = back[:, own + 3 * img :].reshape(samples, heads, 3, txt, head)
    return (img_out, txt_out, img_grad, txt_grad, gain_grad)


def solution(mesh):
    rows = P(("grp", "dp"), None, "seq", None)
    grads = P(("grp", "dp"), None, None, "seq", None)
    return jax.shard_map(
        per_device,
        mesh=mesh,
        in_specs=(grads, grads, rows, rows, P(("grp", "dp")), P()),
        out_specs=(rows, rows, grads, grads, P()),
        check_vma=False,
    )
```

```python
import functools
import math

import jax
import jax.numpy as jnp
from jax import lax
from jax.experimental import pallas as pl
from jax.experimental.pallas import tpu as pltpu
from jax.sharding import PartitionSpec as P

F32 = jnp.float32
BF16 = jnp.bfloat16
EPS = 1e-06
GROUP = 8
KEY_TILE = 512
SPARE_ROWS = 16


def inverse_rms(values):
    return lax.rsqrt(jnp.mean(values * values, axis=-1, keepdims=True) + EPS)


def norm_backward(values, gain, upstream):
    inverse = inverse_rms(values)
    scaled = gain * upstream
    inner = jnp.mean(scaled * values, axis=-1, keepdims=True)
    grad = inverse * scaled - values * (inverse * inverse * inverse * inner)
    return grad, upstream * values * inverse


def pair_kernel(img, txt, values_part, length_ref, gains_ref, in_ref, out_ref, *rest):
    if values_part:
        kn_ref, vaug_ref, eb_ref, acc_ref = rest
    else:
        terms_ref, kn_ref, vaug_ref, eb_ref, acc_ref = rest
    devices = in_ref.shape[0]
    head = in_ref.shape[2]
    blocks = devices // GROUP
    img_block, txt_block = GROUP * img, GROUP * txt
    block = img_block + txt_block
    full = blocks * block
    tile = math.gcd(KEY_TILE, full)
    scale = 1.0 / math.sqrt(head)
    to_exp2 = scale * math.log2(math.e)
    in_txt = 3 * img
    in_cot = 3 * (img + txt)
    out_dv = img + txt
    out_txt = 2 * img
    length = length_ref[0]

    def load(b, img_at, txt_at):
        rows = pl.ds(b * GROUP, GROUP)
        return jnp.concatenate(
            [
                in_ref[rows, img_at : img_at + img].reshape(img_block, head),
                in_ref[rows, txt_at : txt_at + txt].reshape(txt_block, head),
            ],
            axis=0,
        )

    def store(b, img_at, txt_at, values):
        rows = pl.ds(b * GROUP, GROUP)
        out_ref[rows, img_at : img_at + img] = values[:img_block].reshape(GROUP, img, head)
        out_ref[rows, txt_at : txt_at + txt] = values[img_block:].reshape(GROUP, txt, head)

    def gain_rows(which):
        is_img = lax.broadcasted_iota(jnp.int32, (block, head), 0) < img_block
        return jnp.where(is_img, gains_ref[which : which + 1], gains_ref[which + 2 : which + 3])

    def live_rows(b):
        row = lax.broadcasted_iota(jnp.int32, (block, head), 0)
        return jnp.logical_or(row < img_block, row - img_block + b * txt_block < length)

    def add_terms(which, terms):
        terms_ref[which : which + 1] += jnp.sum(terms[:img_block], axis=0, keepdims=True)
        terms_ref[which + 2 : which + 3] += jnp.sum(terms[img_block:], axis=0, keepdims=True)

    acc_ref[...] = jnp.zeros_like(acc_ref)
    if not values_part:
        terms_ref[...] = jnp.zeros_like(terms_ref)

    for b in range(blocks):
        at = slice(b * block, (b + 1) * block)
        live = live_rows(b)
        raw = load(b, img, in_txt + txt).astype(F32)
        normed = raw * inverse_rms(raw) * gain_rows(1)
        kn_ref[at, :] = jnp.where(live, normed, 0.0).astype(BF16)
        values = load(b, 2 * img, in_txt + 2 * txt).astype(F32)
        vaug_ref[at, :head] = jnp.where(live, values, 0.0).astype(BF16)
        vaug_ref[at, head:] = jnp.where(live, 1.0, 0.0).astype(BF16)

    by_rows = (((1,), (1,)), ((), ()))

    def forward(b, held):
        raw = load(b, 0, in_txt).astype(F32)
        gain = gain_rows(0)
        qn = (raw * inverse_rms(raw) * gain).astype(BF16)
        summed = jnp.zeros((block, 2 * head), F32)
        for start in range(0, full, tile):
            keys = slice(start, start + tile)
            scores = lax.dot_general(qn, kn_ref[keys, :], by_rows, preferred_element_type=F32)
            expo = jnp.exp2(scores * to_exp2).astype(BF16)
            held[:, keys] = expo
            summed += jnp.dot(expo, vaug_ref[keys, :], preferred_element_type=F32)
        per_total = 1.0 / summed[:, head:]
        return raw, gain, qn, summed[:, :head] * per_total, per_total

    def values_backward(b, held, raw, gain, qn, out, per_total):
        store(b, 0, img, out.astype(BF16))
        cot32 = load(b, in_cot, in_cot + img).astype(F32)
        cot_t = jnp.transpose((cot32 * per_total).astype(BF16))
        for start in range(0, full, tile):
            keys = slice(start, start + tile)
            acc_ref[:, keys] += jnp.dot(cot_t, held[:, keys], preferred_element_type=F32)

    def scores_backward(b, held, raw, gain, qn, out, per_total):
        cot = load(b, in_cot, in_cot + img)
        delta = jnp.sum(out * cot.astype(F32), axis=-1, keepdims=True)
        qn_t = jnp.transpose((qn.astype(F32) * (per_total * scale)).astype(BF16))
        dq = jnp.zeros((block, head), F32)
        for start in range(0, full, tile):
            keys = slice(start, start + tile)
            dprobs = lax.dot_general(
                cot, vaug_ref[keys, :head], by_rows, preferred_element_type=F32
            )
            dscores = held[:, keys] * (dprobs - delta).astype(BF16)
            dq += jnp.dot(dscores, kn_ref[keys, :], preferred_element_type=F32)
            acc_ref[:, keys] += jnp.dot(qn_t, dscores, preferred_element_type=F32)
        grad, terms = norm_backward(raw, gain, dq * (per_total * scale))
        store(b, 0, out_txt, grad.astype(BF16))
        add_terms(0, terms)

    backward = values_backward if values_part else scores_backward

    @pl.loop(0, blocks, step=2)
    def _queries(b):
        first = forward(b, eb_ref.at[0])
        second = forward(b + 1, eb_ref.at[1])
        backward(b, eb_ref.at[0], *first)
        backward(b + 1, eb_ref.at[1], *second)

    @pl.loop(0, blocks)
    def _key_grads(b):
        at = pl.ds(pl.multiple_of(b * block, block), block)
        upstream = jnp.where(live_rows(b), jnp.transpose(acc_ref[:, at]), 0.0)
        if values_part:
            store(b, out_dv, out_dv + img, upstream.astype(BF16))
        else:
            raw = load(b, img, in_txt + txt).astype(F32)
            grad, terms = norm_backward(raw, gain_rows(1), upstream)
            store(b, img, out_txt + txt, grad.astype(BF16))
            add_terms(1, terms)


def attend_pair(arrived, length, gains, img, txt, values_part, spare_rows):
    devices, _, head = arrived.shape
    rows = 2 * (img + txt) + spare_rows
    full = devices * (img + txt)
    block = GROUP * (img + txt)
    in_vmem = pl.BlockSpec(memory_space=pltpu.VMEM)
    out_shape = [jax.ShapeDtypeStruct((devices, rows, head), BF16)]
    if not values_part:
        out_shape.append(jax.ShapeDtypeStruct((4, head), F32))
    return pl.pallas_call(
        functools.partial(pair_kernel, img, txt, values_part),
        out_shape=out_shape,
        in_specs=[pl.BlockSpec(memory_space=pltpu.SMEM), in_vmem, in_vmem],
        out_specs=[in_vmem] * len(out_shape),
        scratch_shapes=[
            pltpu.VMEM((full, head), BF16),
            pltpu.VMEM((full, 2 * head), BF16),
            pltpu.VMEM((2, block, full), BF16),
            pltpu.VMEM((head, full), F32),
        ],
        compiler_params=pltpu.CompilerParams(vmem_limit_bytes=40 * 1024 * 1024),
        cost_estimate=pl.CostEstimate(
            flops=(6 if values_part else 10) * full * full * head,
            bytes_accessed=4 * devices * rows * head,
            transcendentals=full * full,
        ),
        name="attend_values" if values_part else "attend_scores",
    )(length, gains, arrived)


def pack_kernel(*refs):
    *parts, out_ref = refs
    at = 0
    for part in parts:
        rows = part.shape[1]
        out_ref[:, at : at + rows] = part[...]
        at += rows


def pack_rows(*parts):
    pairs, _, head = parts[0].shape
    rows = sum(part.shape[1] for part in parts)
    step = pairs // 4
    return pl.pallas_call(
        pack_kernel,
        out_shape=jax.ShapeDtypeStruct((pairs, rows, head), BF16),
        grid=(pairs // step,),
        in_specs=[pl.BlockSpec((step, part.shape[1], head), lambda i: (i, 0, 0)) for part in parts],
        out_specs=pl.BlockSpec((step, rows, head), lambda i: (i, 0, 0)),
        name="pack_rows",
    )(*parts)


def split_exact(term):
    high = lax.reduce_precision(term, 8, 7)
    middle = lax.reduce_precision(term - high, 8, 7)
    low = term - high - middle
    return jnp.concatenate([high, middle, low], axis=0).astype(BF16)


def sum_pairwise(term, axis, steps):
    count = lax.axis_size(axis)
    for step in steps:
        term = term + lax.ppermute(term, axis, [(i, i ^ step) for i in range(count)])
    return term


def powers_of_two(count):
    return [1 << bit for bit in range(count.bit_length() - 1)]


def per_device(img_qkv, txt_qkv, img_cot, txt_cot, lengths, norm_gains):
    samples, heads, _, img, head = img_qkv.shape
    txt = txt_qkv.shape[3]
    pairs = samples * heads
    devices = lax.axis_size("seq")
    assert pairs == devices
    outgoing = pack_rows(
        img_qkv.reshape(pairs, 3 * img, head),
        txt_qkv.reshape(pairs, 3 * txt, head),
        img_cot.reshape(pairs, img, head),
        txt_cot.reshape(pairs, txt, head),
    )
    arrived = lax.all_to_all(outgoing, "seq", split_axis=0, concat_axis=0, tiled=True)
    sample = lax.axis_index("seq") // heads
    length = lax.dynamic_slice_in_dim(lengths, sample, 1, 0)
    (values_out,) = attend_pair(arrived, length, norm_gains, img, txt, True, 0)
    values_out, arrived = lax.optimization_barrier((values_out, arrived))
    values_back = lax.all_to_all(values_out, "seq", split_axis=0, concat_axis=0, tiled=True)
    scores_out, terms = attend_pair(arrived, length, norm_gains, img, txt, False, SPARE_ROWS)
    for axis in ("grp", "dp"):
        terms = sum_pairwise(terms, axis, powers_of_two(lax.axis_size(axis)))
    own = img + txt
    split = split_exact(terms)
    split = jnp.pad(split, ((0, SPARE_ROWS - split.shape[0]), (0, 0)))
    scores_out = lax.dynamic_update_slice(
        scores_out, jnp.broadcast_to(split[None], (devices,) + split.shape), (0, 2 * own, 0)
    )
    scores_back = lax.all_to_all(scores_out, "seq", split_axis=0, concat_axis=0, tiled=True)
    group_terms = scores_back[:, 2 * own : 2 * own + 12].astype(F32)
    gain_grad = jnp.sum(group_terms.reshape(devices, 3, 4, head), axis=(0, 1))

    def in_samples(rows):
        return rows.reshape(samples, heads, -1, rows.shape[1], head)

    img_out = in_samples(values_back[:, :img])[:, :, 0]
    txt_out = in_samples(values_back[:, img:own])[:, :, 0]
    img_grad = jnp.concatenate(
        [scores_back[:, : 2 * img], values_back[:, own : own + img]], axis=1
    ).reshape(samples, heads, 3, img, head)
    txt_grad = jnp.concatenate(
        [scores_back[:, 2 * img : 2 * own], values_back[:, own + img :]], axis=1
    ).reshape(samples, heads, 3, txt, head)
    return (img_out, txt_out, img_grad, txt_grad, gain_grad)


def solution(mesh):
    rows = P(("grp", "dp"), None, "seq", None)
    grads = P(("grp", "dp"), None, None, "seq", None)
    return jax.shard_map(
        per_device,
        mesh=mesh,
        in_specs=(grads, grads, rows, rows, P(("grp", "dp")), P()),
        out_specs=(rows, rows, grads, grads, P()),
        check_vma=False,
    )
```

```python
import functools
import math

import jax
import jax.numpy as jnp
from jax import lax
from jax.experimental import pallas as pl
from jax.experimental.pallas import tpu as pltpu
from jax.sharding import PartitionSpec as P

F32 = jnp.float32
BF16 = jnp.bfloat16
EPS = 1e-06
GROUP = 8
KEY_TILE = 512
SPARE_ROWS = 8


def inverse_rms(values):
    return lax.rsqrt(jnp.mean(values * values, axis=-1, keepdims=True) + EPS)


def norm_backward(values, gain, upstream):
    inverse = inverse_rms(values)
    scaled = gain * upstream
    inner = jnp.mean(scaled * values, axis=-1, keepdims=True)
    grad = inverse * scaled - values * (inverse * inverse * inverse * inner)
    return grad, upstream * values * inverse


def pair_kernel(img, txt, values_part, length_ref, gains_ref, in_ref, out_ref, *rest):
    if values_part:
        kn_ref, vaug_ref, eb_ref, acc_ref = rest
    else:
        terms_ref, kn_ref, vaug_ref, eb_ref, acc_ref = rest
    devices = in_ref.shape[0]
    head = in_ref.shape[2]
    blocks = devices // GROUP
    img_block, txt_block = GROUP * img, GROUP * txt
    block = img_block + txt_block
    full = blocks * block
    tile = math.gcd(KEY_TILE, full)
    scale = 1.0 / math.sqrt(head)
    to_exp2 = scale * math.log2(math.e)
    in_txt = 3 * img
    in_cot = 3 * (img + txt)
    out_dv = img + txt
    out_txt = 2 * img
    length = length_ref[0]

    def load(b, img_at, txt_at):
        rows = pl.ds(b * GROUP, GROUP)
        return jnp.concatenate(
            [
                in_ref[rows, img_at : img_at + img].reshape(img_block, head),
                in_ref[rows, txt_at : txt_at + txt].reshape(txt_block, head),
            ],
            axis=0,
        )

    def store(b, img_at, txt_at, values):
        rows = pl.ds(b * GROUP, GROUP)
        out_ref[rows, img_at : img_at + img] = values[:img_block].reshape(GROUP, img, head)
        out_ref[rows, txt_at : txt_at + txt] = values[img_block:].reshape(GROUP, txt, head)

    def gain_rows(which):
        is_img = lax.broadcasted_iota(jnp.int32, (block, head), 0) < img_block
        return jnp.where(is_img, gains_ref[which : which + 1], gains_ref[which + 2 : which + 3])

    def live_rows(b):
        row = lax.broadcasted_iota(jnp.int32, (block, head), 0)
        return jnp.logical_or(row < img_block, row - img_block + b * txt_block < length)

    def add_terms(which, terms):
        terms_ref[which : which + 1] += jnp.sum(terms[:img_block], axis=0, keepdims=True)
        terms_ref[which + 2 : which + 3] += jnp.sum(terms[img_block:], axis=0, keepdims=True)

    acc_ref[...] = jnp.zeros_like(acc_ref)
    if not values_part:
        terms_ref[...] = jnp.zeros_like(terms_ref)

    for b in range(blocks):
        at = slice(b * block, (b + 1) * block)
        live = live_rows(b)
        raw = load(b, img, in_txt + txt).astype(F32)
        normed = raw * inverse_rms(raw) * gain_rows(1)
        kn_ref[at, :] = jnp.where(live, normed, 0.0).astype(BF16)
        values = load(b, 2 * img, in_txt + 2 * txt).astype(F32)
        vaug_ref[at, :head] = jnp.where(live, values, 0.0).astype(BF16)
        vaug_ref[at, head:] = jnp.where(live, 1.0, 0.0).astype(BF16)

    by_rows = (((1,), (1,)), ((), ()))

    def forward(b, held):
        raw = load(b, 0, in_txt).astype(F32)
        gain = gain_rows(0)
        qn = (raw * inverse_rms(raw) * gain).astype(BF16)
        summed = jnp.zeros((block, 2 * head), F32)
        for start in range(0, full, tile):
            keys = slice(start, start + tile)
            scores = lax.dot_general(qn, kn_ref[keys, :], by_rows, preferred_element_type=F32)
            expo = jnp.exp2(scores * to_exp2).astype(BF16)
            held[:, keys] = expo
            summed += jnp.dot(expo, vaug_ref[keys, :], preferred_element_type=F32)
        per_total = 1.0 / summed[:, head:]
        return raw, gain, qn, summed[:, :head] * per_total, per_total

    def values_backward(b, held, raw, gain, qn, out, per_total):
        store(b, 0, img, out.astype(BF16))
        cot32 = load(b, in_cot, in_cot + img).astype(F32)
        cot_t = jnp.transpose((cot32 * per_total).astype(BF16))
        for start in range(0, full, tile):
            keys = slice(start, start + tile)
            acc_ref[:, keys] += jnp.dot(cot_t, held[:, keys], preferred_element_type=F32)

    def scores_backward(b, held, raw, gain, qn, out, per_total):
        cot = load(b, in_cot, in_cot + img)
        delta = jnp.sum(out * cot.astype(F32), axis=-1, keepdims=True)
        qn_t = jnp.transpose((qn.astype(F32) * (per_total * scale)).astype(BF16))
        dq = jnp.zeros((block, head), F32)
        for start in range(0, full, tile):
            keys = slice(start, start + tile)
            dprobs = lax.dot_general(
                cot, vaug_ref[keys, :head], by_rows, preferred_element_type=F32
            )
            dscores = held[:, keys] * (dprobs - delta).astype(BF16)
            dq += jnp.dot(dscores, kn_ref[keys, :], preferred_element_type=F32)
            acc_ref[:, keys] += jnp.dot(qn_t, dscores, preferred_element_type=F32)
        grad, terms = norm_backward(raw, gain, dq * (per_total * scale))
        store(b, 0, out_txt, grad.astype(BF16))
        add_terms(0, terms)

    if values_part:
        held = [eb_ref.at[b] for b in range(blocks)]
        results = [forward(0, held[0])]
        for b in range(blocks):
            if b + 1 < blocks:
                results.append(forward(b + 1, held[b + 1]))
            values_backward(b, held[b], *results[b])
        for b in range(blocks):
            at = slice(b * block, (b + 1) * block)
            col = lax.broadcasted_iota(jnp.int32, (head, block), 1)
            live = jnp.logical_or(col < img_block, col - img_block + b * txt_block < length)
            dv_t = jnp.where(live, acc_ref[:, at], 0.0).astype(BF16)
            store(b, out_dv, out_dv + img, jnp.transpose(dv_t))
        return

    @pl.loop(0, blocks, step=2)
    def _queries(b):
        first = forward(b, eb_ref.at[0])
        second = forward(b + 1, eb_ref.at[1])
        scores_backward(b, eb_ref.at[0], *first)
        scores_backward(b + 1, eb_ref.at[1], *second)

    @pl.loop(0, blocks)
    def _key_grads(b):
        at = pl.ds(pl.multiple_of(b * block, block), block)
        upstream = jnp.where(live_rows(b), jnp.transpose(acc_ref[:, at]), 0.0)
        raw = load(b, img, in_txt + txt).astype(F32)
        grad, terms = norm_backward(raw, gain_rows(1), upstream)
        store(b, img, out_txt + txt, grad.astype(BF16))
        add_terms(1, terms)


def attend_pair(arrived, length, gains, img, txt, values_part, spare_rows):
    devices, _, head = arrived.shape
    rows = 2 * (img + txt) + spare_rows
    full = devices * (img + txt)
    block = GROUP * (img + txt)
    in_vmem = pl.BlockSpec(memory_space=pltpu.VMEM)
    out_shape = [jax.ShapeDtypeStruct((devices, rows, head), BF16)]
    if not values_part:
        out_shape.append(jax.ShapeDtypeStruct((4, head), F32))
    return pl.pallas_call(
        functools.partial(pair_kernel, img, txt, values_part),
        out_shape=out_shape,
        in_specs=[pl.BlockSpec(memory_space=pltpu.SMEM), in_vmem, in_vmem],
        out_specs=[in_vmem] * len(out_shape),
        scratch_shapes=[
            pltpu.VMEM((full, head), BF16),
            pltpu.VMEM((full, 2 * head), BF16),
            pltpu.VMEM((full // block if values_part else 2, block, full), BF16),
            pltpu.VMEM((head, full), F32),
        ],
        compiler_params=pltpu.CompilerParams(vmem_limit_bytes=40 * 1024 * 1024),
        cost_estimate=pl.CostEstimate(
            flops=(6 if values_part else 10) * full * full * head,
            bytes_accessed=4 * devices * rows * head,
            transcendentals=full * full,
        ),
        name="attend_values" if values_part else "attend_scores",
    )(length, gains, arrived)


def split_rows(term):
    high = lax.reduce_precision(term, 8, 7)
    return jnp.concatenate([high, term - high], axis=0).astype(BF16)


def sum_pairwise(term, axis, steps):
    count = lax.axis_size(axis)
    for step in steps:
        term = term + lax.ppermute(term, axis, [(i, i ^ step) for i in range(count)])
    return term


def powers_of_two(count):
    return [1 << bit for bit in range(count.bit_length() - 1)]


def per_device(img_qkv, txt_qkv, img_cot, txt_cot, lengths, norm_gains):
    samples, heads, _, img, head = img_qkv.shape
    txt = txt_qkv.shape[3]
    pairs = samples * heads
    devices = lax.axis_size("seq")
    assert pairs == devices
    outgoing = jnp.concatenate(
        [
            img_qkv.reshape(pairs, 3 * img, head),
            txt_qkv.reshape(pairs, 3 * txt, head),
            img_cot.reshape(pairs, img, head),
            txt_cot.reshape(pairs, txt, head),
        ],
        axis=1,
    )
    arrived = lax.all_to_all(outgoing, "seq", split_axis=0, concat_axis=0, tiled=True)
    sample = lax.axis_index("seq") // heads
    length = lax.dynamic_slice_in_dim(lengths, sample, 1, 0)
    (values_out,) = attend_pair(arrived, length, norm_gains, img, txt, True, 0)
    values_out, arrived = lax.optimization_barrier((values_out, arrived))
    values_back = lax.all_to_all(values_out, "seq", split_axis=0, concat_axis=0, tiled=True)
    scores_out, terms = attend_pair(arrived, length, norm_gains, img, txt, False, SPARE_ROWS)
    for axis in ("grp", "dp"):
        terms = sum_pairwise(terms, axis, powers_of_two(lax.axis_size(axis)))
    own = img + txt
    split = split_rows(terms)
    scores_out = lax.dynamic_update_slice(
        scores_out, jnp.broadcast_to(split[None], (devices,) + split.shape), (0, 2 * own, 0)
    )
    scores_back = lax.all_to_all(scores_out, "seq", split_axis=0, concat_axis=0, tiled=True)
    group_terms = jnp.sum(scores_back[:, 2 * own :].astype(F32), axis=0)
    gain_grad = group_terms[:4] + group_terms[4:]

    def in_samples(rows):
        return rows.reshape(samples, heads, -1, rows.shape[1], head)

    img_out = in_samples(values_back[:, :img])[:, :, 0]
    txt_out = in_samples(values_back[:, img:own])[:, :, 0]
    img_grad = jnp.concatenate(
        [scores_back[:, : 2 * img], values_back[:, own : own + img]], axis=1
    ).reshape(samples, heads, 3, img, head)
    txt_grad = jnp.concatenate(
        [scores_back[:, 2 * img : 2 * own], values_back[:, own + img :]], axis=1
    ).reshape(samples, heads, 3, txt, head)
    return (img_out, txt_out, img_grad, txt_grad, gain_grad)


def solution(mesh):
    rows = P(("grp", "dp"), None, "seq", None)
    grads = P(("grp", "dp"), None, None, "seq", None)
    return jax.shard_map(
        per_device,
        mesh=mesh,
        in_specs=(grads, grads, rows, rows, P(("grp", "dp")), P()),
        out_specs=(rows, rows, grads, grads, P()),
        check_vma=False,
    )
```

```python
import functools
import math

import jax
import jax.numpy as jnp
from jax import lax
from jax.experimental import pallas as pl
from jax.experimental.pallas import tpu as pltpu
from jax.sharding import PartitionSpec as P

F32 = jnp.float32
BF16 = jnp.bfloat16
EPS = 1e-06
GROUP = 8
PACK_CHUNKS = 4
SPARE_ROWS = 8


def inverse_rms(values):
    return lax.rsqrt(jnp.mean(values * values, axis=-1, keepdims=True) + EPS)


def norm_backward(values, gain, upstream):
    inverse = inverse_rms(values)
    scaled = gain * upstream
    inner = jnp.mean(scaled * values, axis=-1, keepdims=True)
    grad = inverse * scaled - values * (inverse * inverse * inverse * inner)
    return grad, upstream * values * inverse


def pair_kernel(img, txt, values_part, length_ref, gains_ref, in_ref, out_ref, *rest):
    if values_part:
        kn_ref, vaug_ref, eb_ref, acc_ref = rest
    else:
        terms_ref, kn_ref, vaug_ref, eb_ref, acc_ref = rest
    devices = in_ref.shape[0]
    head = in_ref.shape[2]
    blocks = devices // GROUP
    img_block, txt_block = GROUP * img, GROUP * txt
    block = img_block + txt_block
    full = blocks * block
    tile = math.gcd(1024 if values_part else 512, full)
    scale = 1.0 / math.sqrt(head)
    to_exp2 = scale * math.log2(math.e)
    in_txt = 3 * img
    in_cot = 3 * (img + txt)
    out_dv = img + txt
    out_txt = 2 * img
    length = length_ref[0]

    def load(b, img_at, txt_at):
        rows = pl.ds(b * GROUP, GROUP)
        return jnp.concatenate(
            [
                in_ref[rows, img_at : img_at + img].reshape(img_block, head),
                in_ref[rows, txt_at : txt_at + txt].reshape(txt_block, head),
            ],
            axis=0,
        )

    def store(b, img_at, txt_at, values):
        rows = pl.ds(b * GROUP, GROUP)
        out_ref[rows, img_at : img_at + img] = values[:img_block].reshape(GROUP, img, head)
        out_ref[rows, txt_at : txt_at + txt] = values[img_block:].reshape(GROUP, txt, head)

    def gain_rows(which):
        is_img = lax.broadcasted_iota(jnp.int32, (block, head), 0) < img_block
        return jnp.where(is_img, gains_ref[which : which + 1], gains_ref[which + 2 : which + 3])

    def live_rows(b):
        row = lax.broadcasted_iota(jnp.int32, (block, head), 0)
        return jnp.logical_or(row < img_block, row - img_block + b * txt_block < length)

    def add_terms(which, terms):
        terms_ref[which : which + 1] += jnp.sum(terms[:img_block], axis=0, keepdims=True)
        terms_ref[which + 2 : which + 3] += jnp.sum(terms[img_block:], axis=0, keepdims=True)

    acc_ref[...] = jnp.zeros_like(acc_ref)
    if not values_part:
        terms_ref[...] = jnp.zeros_like(terms_ref)

    for b in range(blocks):
        at = slice(b * block, (b + 1) * block)
        live = live_rows(b)
        raw = load(b, img, in_txt + txt).astype(F32)
        normed = raw * inverse_rms(raw) * gain_rows(1)
        kn_ref[at, :] = jnp.where(live, normed, 0.0).astype(BF16)
        values = load(b, 2 * img, in_txt + 2 * txt).astype(F32)
        vaug_ref[at, :head] = jnp.where(live, values, 0.0).astype(BF16)
        vaug_ref[at, head:] = jnp.where(live, 1.0, 0.0).astype(BF16)

    by_rows = (((1,), (1,)), ((), ()))

    def forward(b, held):
        raw = load(b, 0, in_txt).astype(F32)
        gain = gain_rows(0)
        qn = (raw * inverse_rms(raw) * gain).astype(BF16)
        summed = jnp.zeros((block, 2 * head), F32)
        for start in range(0, full, tile):
            keys = slice(start, start + tile)
            scores = lax.dot_general(qn, kn_ref[keys, :], by_rows, preferred_element_type=F32)
            expo = jnp.exp2(scores * to_exp2).astype(BF16)
            held[:, keys] = expo
            summed += jnp.dot(expo, vaug_ref[keys, :], preferred_element_type=F32)
        per_total = 1.0 / summed[:, head:]
        return raw, gain, qn, summed[:, :head] * per_total, per_total

    def values_backward(b, held, raw, gain, qn, out, per_total):
        store(b, 0, img, out.astype(BF16))
        cot32 = load(b, in_cot, in_cot + img).astype(F32)
        cot_t = jnp.transpose((cot32 * per_total).astype(BF16))
        for start in range(0, full, tile):
            keys = slice(start, start + tile)
            acc_ref[:, keys] += jnp.dot(cot_t, held[:, keys], preferred_element_type=F32)

    def scores_backward(b, held, raw, gain, qn, out, per_total):
        cot = load(b, in_cot, in_cot + img)
        delta = jnp.sum(out * cot.astype(F32), axis=-1, keepdims=True)
        qn_t = jnp.transpose((qn.astype(F32) * (per_total * scale)).astype(BF16))
        dq = jnp.zeros((block, head), F32)
        for start in range(0, full, tile):
            keys = slice(start, start + tile)
            dprobs = lax.dot_general(
                cot, vaug_ref[keys, :head], by_rows, preferred_element_type=F32
            )
            dscores = held[:, keys] * (dprobs - delta).astype(BF16)
            dq += jnp.dot(dscores, kn_ref[keys, :], preferred_element_type=F32)
            acc_ref[:, keys] += jnp.dot(qn_t, dscores, preferred_element_type=F32)
        grad, terms = norm_backward(raw, gain, dq * (per_total * scale))
        store(b, 0, out_txt, grad.astype(BF16))
        add_terms(0, terms)

    if values_part:
        held = [eb_ref.at[b] for b in range(blocks)]
        results = [forward(0, held[0])]
        for b in range(blocks):
            if b + 1 < blocks:
                results.append(forward(b + 1, held[b + 1]))
            values_backward(b, held[b], *results[b])
        for b in range(blocks):
            at = slice(b * block, (b + 1) * block)
            col = lax.broadcasted_iota(jnp.int32, (head, block), 1)
            live = jnp.logical_or(col < img_block, col - img_block + b * txt_block < length)
            dv_t = jnp.where(live, acc_ref[:, at], 0.0).astype(BF16)
            store(b, out_dv, out_dv + img, jnp.transpose(dv_t))
        return

    @pl.loop(0, blocks, step=2)
    def _queries(b):
        first = forward(b, eb_ref.at[0])
        second = forward(b + 1, eb_ref.at[1])
        scores_backward(b, eb_ref.at[0], *first)
        scores_backward(b + 1, eb_ref.at[1], *second)

    @pl.loop(0, blocks)
    def _key_grads(b):
        at = pl.ds(pl.multiple_of(b * block, block), block)
        upstream = jnp.where(live_rows(b), jnp.transpose(acc_ref[:, at]), 0.0)
        raw = load(b, img, in_txt + txt).astype(F32)
        grad, terms = norm_backward(raw, gain_rows(1), upstream)
        store(b, img, out_txt + txt, grad.astype(BF16))
        add_terms(1, terms)


def attend_pair(arrived, length, gains, img, txt, values_part, spare_rows):
    devices, _, head = arrived.shape
    rows = 2 * (img + txt) + spare_rows
    full = devices * (img + txt)
    block = GROUP * (img + txt)
    in_vmem = pl.BlockSpec(memory_space=pltpu.VMEM)
    out_shape = [jax.ShapeDtypeStruct((devices, rows, head), BF16)]
    if not values_part:
        out_shape.append(jax.ShapeDtypeStruct((4, head), F32))
    return pl.pallas_call(
        functools.partial(pair_kernel, img, txt, values_part),
        out_shape=out_shape,
        in_specs=[pl.BlockSpec(memory_space=pltpu.SMEM), in_vmem, in_vmem],
        out_specs=[in_vmem] * len(out_shape),
        scratch_shapes=[
            pltpu.VMEM((full, head), BF16),
            pltpu.VMEM((full, 2 * head), BF16),
            pltpu.VMEM((full // block if values_part else 2, block, full), BF16),
            pltpu.VMEM((head, full), F32),
        ],
        compiler_params=pltpu.CompilerParams(vmem_limit_bytes=40 * 1024 * 1024),
        cost_estimate=pl.CostEstimate(
            flops=(6 if values_part else 10) * full * full * head,
            bytes_accessed=4 * devices * rows * head,
            transcendentals=full * full,
        ),
        name="attend_values" if values_part else "attend_scores",
    )(length, gains, arrived)


def pack_kernel(*refs):
    *parts, out_ref, held, in_sems, out_sems = refs
    step = held.shape[0] // PACK_CHUNKS
    arriving = []
    for c in range(PACK_CHUNKS):
        pairs = slice(c * step, (c + 1) * step)
        chunk = []
        at = 0
        for i, part in enumerate(parts):
            rows = slice(at, at + part.shape[1])
            copy = pltpu.make_async_copy(part.at[pairs], held.at[pairs, rows], in_sems.at[c, i])
            copy.start()
            chunk.append(copy)
            at += part.shape[1]
        arriving.append(chunk)
    leaving = []
    for c in range(PACK_CHUNKS):
        pairs = slice(c * step, (c + 1) * step)
        for copy in arriving[c]:
            copy.wait()
        copy = pltpu.make_async_copy(held.at[pairs], out_ref.at[pairs], out_sems.at[c])
        copy.start()
        leaving.append(copy)
    for copy in leaving:
        copy.wait()


def pack_rows(*parts):
    pairs, _, head = parts[0].shape
    rows = sum(part.shape[1] for part in parts)
    return pl.pallas_call(
        pack_kernel,
        out_shape=jax.ShapeDtypeStruct((pairs, rows, head), BF16),
        in_specs=[pl.BlockSpec(memory_space=pl.ANY)] * len(parts),
        out_specs=pl.BlockSpec(memory_space=pl.ANY),
        scratch_shapes=[
            pltpu.VMEM((pairs, rows, head), BF16),
            pltpu.SemaphoreType.DMA((PACK_CHUNKS, len(parts))),
            pltpu.SemaphoreType.DMA((PACK_CHUNKS,)),
        ],
        name="pack_rows",
    )(*parts)


def split_rows(term):
    high = lax.reduce_precision(term, 8, 7)
    return jnp.concatenate([high, term - high], axis=0).astype(BF16)


def sum_pairwise(term, axis, steps):
    count = lax.axis_size(axis)
    for step in steps:
        term = term + lax.ppermute(term, axis, [(i, i ^ step) for i in range(count)])
    return term


def powers_of_two(count):
    return [1 << bit for bit in range(count.bit_length() - 1)]


def per_device(img_qkv, txt_qkv, img_cot, txt_cot, lengths, norm_gains):
    samples, heads, _, img, head = img_qkv.shape
    txt = txt_qkv.shape[3]
    pairs = samples * heads
    devices = lax.axis_size("seq")
    assert pairs == devices
    outgoing = pack_rows(
        img_qkv.reshape(pairs, 3 * img, head),
        txt_qkv.reshape(pairs, 3 * txt, head),
        img_cot.reshape(pairs, img, head),
        txt_cot.reshape(pairs, txt, head),
    )
    arrived = lax.all_to_all(outgoing, "seq", split_axis=0, concat_axis=0, tiled=True)
    sample = lax.axis_index("seq") // heads
    length = lax.dynamic_slice_in_dim(lengths, sample, 1, 0)
    (values_out,) = attend_pair(arrived, length, norm_gains, img, txt, True, 0)
    values_out, arrived = lax.optimization_barrier((values_out, arrived))
    values_back = lax.all_to_all(values_out, "seq", split_axis=0, concat_axis=0, tiled=True)
    scores_out, terms = attend_pair(arrived, length, norm_gains, img, txt, False, SPARE_ROWS)
    for axis in ("grp", "dp"):
        terms = sum_pairwise(terms, axis, powers_of_two(lax.axis_size(axis)))
    own = img + txt
    split = split_rows(terms)
    scores_out = lax.dynamic_update_slice(
        scores_out, jnp.broadcast_to(split[None], (devices,) + split.shape), (0, 2 * own, 0)
    )
    scores_back = lax.all_to_all(scores_out, "seq", split_axis=0, concat_axis=0, tiled=True)
    group_terms = jnp.sum(scores_back[:, 2 * own :].astype(F32), axis=0)
    gain_grad = group_terms[:4] + group_terms[4:]

    def in_samples(rows):
        return rows.reshape(samples, heads, -1, rows.shape[1], head)

    img_out = in_samples(values_back[:, :img])[:, :, 0]
    txt_out = in_samples(values_back[:, img:own])[:, :, 0]
    img_grad = jnp.concatenate(
        [scores_back[:, : 2 * img], values_back[:, own : own + img]], axis=1
    ).reshape(samples, heads, 3, img, head)
    txt_grad = jnp.concatenate(
        [scores_back[:, 2 * img : 2 * own], values_back[:, own + img :]], axis=1
    ).reshape(samples, heads, 3, txt, head)
    return (img_out, txt_out, img_grad, txt_grad, gain_grad)


def solution(mesh):
    rows = P(("grp", "dp"), None, "seq", None)
    grads = P(("grp", "dp"), None, None, "seq", None)
    return jax.shard_map(
        per_device,
        mesh=mesh,
        in_specs=(grads, grads, rows, rows, P(("grp", "dp")), P()),
        out_specs=(rows, rows, grads, grads, P()),
        check_vma=False,
    )
```

```python
import functools
import math

import jax
import jax.numpy as jnp
from jax import lax
from jax.experimental import pallas as pl
from jax.experimental.pallas import tpu as pltpu
from jax.sharding import PartitionSpec as P

F32 = jnp.float32
BF16 = jnp.bfloat16
EPS = 1e-06
GROUP = 8
PACK_CHUNKS = 4
SPARE_ROWS = 8


def inverse_rms(values):
    return lax.rsqrt(jnp.mean(values * values, axis=-1, keepdims=True) + EPS)


def norm_backward(values, gain, upstream):
    inverse = inverse_rms(values)
    scaled = gain * upstream
    inner = jnp.mean(scaled * values, axis=-1, keepdims=True)
    grad = inverse * scaled - values * (inverse * inverse * inverse * inner)
    return grad, upstream * values * inverse


def pair_kernel(img, txt, values_part, length_ref, gains_ref, in_ref, out_ref, *rest):
    if values_part:
        kn_ref, vaug_ref, eb_ref, acc_ref = rest
    else:
        terms_ref, kn_ref, vaug_ref, eb_ref, acc_ref = rest
    devices = in_ref.shape[0]
    head = in_ref.shape[2]
    blocks = devices // GROUP
    img_block, txt_block = GROUP * img, GROUP * txt
    block = img_block + txt_block
    full = blocks * block
    tile = math.gcd(256 if values_part else 512, full)
    scale = 1.0 / math.sqrt(head)
    to_exp2 = scale * math.log2(math.e)
    in_txt = 3 * img
    in_cot = 3 * (img + txt)
    out_dv = img + txt
    out_txt = 2 * img
    length = length_ref[0]

    def load(b, img_at, txt_at):
        rows = pl.ds(b * GROUP, GROUP)
        return jnp.concatenate(
            [
                in_ref[rows, img_at : img_at + img].reshape(img_block, head),
                in_ref[rows, txt_at : txt_at + txt].reshape(txt_block, head),
            ],
            axis=0,
        )

    def store(b, img_at, txt_at, values):
        rows = pl.ds(b * GROUP, GROUP)
        out_ref[rows, img_at : img_at + img] = values[:img_block].reshape(GROUP, img, head)
        out_ref[rows, txt_at : txt_at + txt] = values[img_block:].reshape(GROUP, txt, head)

    def gain_rows(which):
        is_img = lax.broadcasted_iota(jnp.int32, (block, head), 0) < img_block
        return jnp.where(is_img, gains_ref[which : which + 1], gains_ref[which + 2 : which + 3])

    def live_rows(b):
        row = lax.broadcasted_iota(jnp.int32, (block, head), 0)
        return jnp.logical_or(row < img_block, row - img_block + b * txt_block < length)

    def add_terms(which, terms):
        terms_ref[which : which + 1] += jnp.sum(terms[:img_block], axis=0, keepdims=True)
        terms_ref[which + 2 : which + 3] += jnp.sum(terms[img_block:], axis=0, keepdims=True)

    if not values_part:
        acc_ref[...] = jnp.zeros_like(acc_ref)
        terms_ref[...] = jnp.zeros_like(terms_ref)

    for b in range(blocks):
        at = slice(b * block, (b + 1) * block)
        live = live_rows(b)
        raw = load(b, img, in_txt + txt).astype(F32)
        normed = raw * inverse_rms(raw) * gain_rows(1)
        kn_ref[at, :] = jnp.where(live, normed, 0.0).astype(BF16)
        values = load(b, 2 * img, in_txt + 2 * txt).astype(F32)
        vaug_ref[at, :head] = jnp.where(live, values, 0.0).astype(BF16)
        vaug_ref[at, head:] = jnp.where(live, 1.0, 0.0).astype(BF16)

    by_rows = (((1,), (1,)), ((), ()))

    def forward(b, held):
        raw = load(b, 0, in_txt).astype(F32)
        gain = gain_rows(0)
        qn = (raw * inverse_rms(raw) * gain).astype(BF16)
        summed = jnp.zeros((block, 2 * head), F32)
        for start in range(0, full, tile):
            keys = slice(start, start + tile)
            scores = lax.dot_general(qn, kn_ref[keys, :], by_rows, preferred_element_type=F32)
            expo = jnp.exp2(scores * to_exp2).astype(BF16)
            held[:, keys] = expo
            summed += jnp.dot(expo, vaug_ref[keys, :], preferred_element_type=F32)
        per_total = 1.0 / summed[:, head:]
        return raw, gain, qn, summed[:, :head] * per_total, per_total

    def values_backward(b, held, raw, gain, qn, out, per_total):
        store(b, 0, img, out.astype(BF16))
        cot32 = load(b, in_cot, in_cot + img).astype(F32)
        cot_t = jnp.transpose((cot32 * per_total).astype(BF16))
        for start in range(0, full, tile):
            keys = slice(start, start + tile)
            sums = jnp.dot(cot_t, held[:, keys], preferred_element_type=F32)
            acc_ref[:, keys] = sums if b == 0 else acc_ref[:, keys] + sums

    def scores_backward(b, held, raw, gain, qn, out, per_total):
        cot = load(b, in_cot, in_cot + img)
        delta = jnp.sum(out * cot.astype(F32), axis=-1, keepdims=True)
        qn_t = jnp.transpose((qn.astype(F32) * (per_total * scale)).astype(BF16))
        dq = jnp.zeros((block, head), F32)
        for start in range(0, full, tile):
            keys = slice(start, start + tile)
            dprobs = lax.dot_general(
                cot, vaug_ref[keys, :head], by_rows, preferred_element_type=F32
            )
            dscores = held[:, keys] * (dprobs - delta).astype(BF16)
            dq += jnp.dot(dscores, kn_ref[keys, :], preferred_element_type=F32)
            acc_ref[:, keys] += jnp.dot(qn_t, dscores, preferred_element_type=F32)
        grad, terms = norm_backward(raw, gain, dq * (per_total * scale))
        store(b, 0, out_txt, grad.astype(BF16))
        add_terms(0, terms)

    if values_part:
        held = [eb_ref.at[b] for b in range(blocks)]
        results = [forward(0, held[0])]
        for b in range(blocks):
            if b + 1 < blocks:
                results.append(forward(b + 1, held[b + 1]))
            values_backward(b, held[b], *results[b])
        for b in range(blocks):
            at = slice(b * block, (b + 1) * block)
            col = lax.broadcasted_iota(jnp.int32, (head, block), 1)
            live = jnp.logical_or(col < img_block, col - img_block + b * txt_block < length)
            dv_t = jnp.where(live, acc_ref[:, at], 0.0).astype(BF16)
            store(b, out_dv, out_dv + img, jnp.transpose(dv_t))
        return

    @pl.loop(0, blocks, step=2)
    def _queries(b):
        first = forward(b, eb_ref.at[0])
        second = forward(b + 1, eb_ref.at[1])
        scores_backward(b, eb_ref.at[0], *first)
        scores_backward(b + 1, eb_ref.at[1], *second)

    @pl.loop(0, blocks)
    def _key_grads(b):
        at = pl.ds(pl.multiple_of(b * block, block), block)
        upstream = jnp.where(live_rows(b), jnp.transpose(acc_ref[:, at]), 0.0)
        raw = load(b, img, in_txt + txt).astype(F32)
        grad, terms = norm_backward(raw, gain_rows(1), upstream)
        store(b, img, out_txt + txt, grad.astype(BF16))
        add_terms(1, terms)


def attend_pair(arrived, length, gains, img, txt, values_part, spare_rows):
    devices, _, head = arrived.shape
    rows = 2 * (img + txt) + spare_rows
    full = devices * (img + txt)
    block = GROUP * (img + txt)
    in_vmem = pl.BlockSpec(memory_space=pltpu.VMEM)
    out_shape = [jax.ShapeDtypeStruct((devices, rows, head), BF16)]
    if not values_part:
        out_shape.append(jax.ShapeDtypeStruct((4, head), F32))
    return pl.pallas_call(
        functools.partial(pair_kernel, img, txt, values_part),
        out_shape=out_shape,
        in_specs=[pl.BlockSpec(memory_space=pltpu.SMEM), in_vmem, in_vmem],
        out_specs=[in_vmem] * len(out_shape),
        scratch_shapes=[
            pltpu.VMEM((full, head), BF16),
            pltpu.VMEM((full, 2 * head), BF16),
            pltpu.VMEM((full // block if values_part else 2, block, full), BF16),
            pltpu.VMEM((head, full), F32),
        ],
        compiler_params=pltpu.CompilerParams(vmem_limit_bytes=40 * 1024 * 1024),
        cost_estimate=pl.CostEstimate(
            flops=(6 if values_part else 10) * full * full * head,
            bytes_accessed=4 * devices * rows * head,
            transcendentals=full * full,
        ),
        name="attend_values" if values_part else "attend_scores",
    )(length, gains, arrived)


def pack_kernel(*refs):
    *parts, out_ref, held, in_sems, out_sems = refs
    step = held.shape[0] // PACK_CHUNKS
    arriving = []
    for c in range(PACK_CHUNKS):
        pairs = slice(c * step, (c + 1) * step)
        chunk = []
        at = 0
        for i, part in enumerate(parts):
            rows = slice(at, at + part.shape[1])
            copy = pltpu.make_async_copy(part.at[pairs], held.at[pairs, rows], in_sems.at[c, i])
            copy.start()
            chunk.append(copy)
            at += part.shape[1]
        arriving.append(chunk)
    leaving = []
    for c in range(PACK_CHUNKS):
        pairs = slice(c * step, (c + 1) * step)
        for copy in arriving[c]:
            copy.wait()
        copy = pltpu.make_async_copy(held.at[pairs], out_ref.at[pairs], out_sems.at[c])
        copy.start()
        leaving.append(copy)
    for copy in leaving:
        copy.wait()


def pack_rows(*parts):
    pairs, _, head = parts[0].shape
    rows = sum(part.shape[1] for part in parts)
    return pl.pallas_call(
        pack_kernel,
        out_shape=jax.ShapeDtypeStruct((pairs, rows, head), BF16),
        in_specs=[pl.BlockSpec(memory_space=pl.ANY)] * len(parts),
        out_specs=pl.BlockSpec(memory_space=pl.ANY),
        scratch_shapes=[
            pltpu.VMEM((pairs, rows, head), BF16),
            pltpu.SemaphoreType.DMA((PACK_CHUNKS, len(parts))),
            pltpu.SemaphoreType.DMA((PACK_CHUNKS,)),
        ],
        name="pack_rows",
    )(*parts)


def join_kernel(img, txt, values_ref, scores_ref, img_ref, txt_ref, sems):
    own = img + txt
    copies = [
        pltpu.make_async_copy(source, target, sems.at[i])
        for i, (source, target) in enumerate(
            [
                (scores_ref.at[:, : 2 * img], img_ref.at[:, : 2 * img]),
                (values_ref.at[:, own : own + img], img_ref.at[:, 2 * img :]),
                (scores_ref.at[:, 2 * img : 2 * own], txt_ref.at[:, : 2 * txt]),
                (values_ref.at[:, own + img :], txt_ref.at[:, 2 * txt :]),
            ]
        )
    ]
    for copy in copies:
        copy.start()
    for copy in copies:
        copy.wait()


def join_grads(values, scores, img, txt):
    pairs, _, head = values.shape
    return pl.pallas_call(
        functools.partial(join_kernel, img, txt),
        out_shape=[
            jax.ShapeDtypeStruct((pairs, 3 * img, head), BF16),
            jax.ShapeDtypeStruct((pairs, 3 * txt, head), BF16),
        ],
        in_specs=[pl.BlockSpec(memory_space=pltpu.VMEM)] * 2,
        out_specs=[pl.BlockSpec(memory_space=pl.ANY)] * 2,
        scratch_shapes=[pltpu.SemaphoreType.DMA((4,))],
        compiler_params=pltpu.CompilerParams(vmem_limit_bytes=16 * 1024 * 1024),
        name="join_grads",
    )(values, scores)


def split_rows(term):
    high = lax.reduce_precision(term, 8, 7)
    return jnp.concatenate([high, term - high], axis=0).astype(BF16)


def sum_pairwise(term, axis, steps):
    count = lax.axis_size(axis)
    for step in steps:
        term = term + lax.ppermute(term, axis, [(i, i ^ step) for i in range(count)])
    return term


def powers_of_two(count):
    return [1 << bit for bit in range(count.bit_length() - 1)]


def per_device(img_qkv, txt_qkv, img_cot, txt_cot, lengths, norm_gains):
    samples, heads, _, img, head = img_qkv.shape
    txt = txt_qkv.shape[3]
    pairs = samples * heads
    devices = lax.axis_size("seq")
    assert pairs == devices
    outgoing = pack_rows(
        img_qkv.reshape(pairs, 3 * img, head),
        txt_qkv.reshape(pairs, 3 * txt, head),
        img_cot.reshape(pairs, img, head),
        txt_cot.reshape(pairs, txt, head),
    )
    arrived = lax.all_to_all(outgoing, "seq", split_axis=0, concat_axis=0, tiled=True)
    sample = lax.axis_index("seq") // heads
    length = lax.dynamic_slice_in_dim(lengths, sample, 1, 0)
    (values_out,) = attend_pair(arrived, length, norm_gains, img, txt, True, 0)
    values_out, arrived = lax.optimization_barrier((values_out, arrived))
    values_back = lax.all_to_all(values_out, "seq", split_axis=0, concat_axis=0, tiled=True)
    scores_out, terms = attend_pair(arrived, length, norm_gains, img, txt, False, SPARE_ROWS)
    for axis in ("grp", "dp"):
        terms = sum_pairwise(terms, axis, powers_of_two(lax.axis_size(axis)))
    own = img + txt
    split = split_rows(terms)
    scores_out = lax.dynamic_update_slice(
        scores_out, jnp.broadcast_to(split[None], (devices,) + split.shape), (0, 2 * own, 0)
    )
    scores_back = lax.all_to_all(scores_out, "seq", split_axis=0, concat_axis=0, tiled=True)
    group_terms = jnp.sum(scores_back[:, 2 * own :].astype(F32), axis=0)
    gain_grad = group_terms[:4] + group_terms[4:]

    def in_samples(rows):
        return rows.reshape(samples, heads, -1, rows.shape[1], head)

    img_out = in_samples(values_back[:, :img])[:, :, 0]
    txt_out = in_samples(values_back[:, img:own])[:, :, 0]
    img_grad, txt_grad = join_grads(values_back, scores_back, img, txt)
    img_grad = img_grad.reshape(samples, heads, 3, img, head)
    txt_grad = txt_grad.reshape(samples, heads, 3, txt, head)
    return (img_out, txt_out, img_grad, txt_grad, gain_grad)


def solution(mesh):
    rows = P(("grp", "dp"), None, "seq", None)
    grads = P(("grp", "dp"), None, None, "seq", None)
    return jax.shard_map(
        per_device,
        mesh=mesh,
        in_specs=(grads, grads, rows, rows, P(("grp", "dp")), P()),
        out_specs=(rows, rows, grads, grads, P()),
        check_vma=False,
    )
```

```python
import functools
import math

import jax
import jax.numpy as jnp
from jax import lax
from jax.experimental import pallas as pl
from jax.experimental.pallas import tpu as pltpu
from jax.sharding import PartitionSpec as P

F32 = jnp.float32
BF16 = jnp.bfloat16
EPS = 1e-06
GROUP = 8
PACK_CHUNKS = 4
SPARE_ROWS = 8


def inverse_rms(values):
    return lax.rsqrt(jnp.mean(values * values, axis=-1, keepdims=True) + EPS)


def norm_backward(values, gain, upstream):
    inverse = inverse_rms(values)
    scaled = gain * upstream
    inner = jnp.mean(scaled * values, axis=-1, keepdims=True)
    grad = inverse * scaled - values * (inverse * inverse * inverse * inner)
    return grad, upstream * values * inverse


def pair_kernel(img, txt, values_part, length_ref, gains_ref, in_ref, out_ref, *rest):
    if values_part:
        kn_ref, vaug_ref, eb_ref, acc_ref = rest
    else:
        terms_ref, kn_ref, vaug_ref, eb_ref, acc_ref = rest
    devices = in_ref.shape[0]
    head = in_ref.shape[2]
    blocks = devices // GROUP
    img_block, txt_block = GROUP * img, GROUP * txt
    block = img_block + txt_block
    full = blocks * block
    tile = math.gcd(256 if values_part else 512, full)
    scale = 1.0 / math.sqrt(head)
    to_exp2 = scale * math.log2(math.e)
    in_txt = 3 * img
    in_cot = 3 * (img + txt)
    out_dv = img + txt
    out_txt = 2 * img
    length = length_ref[0]

    def load(b, img_at, txt_at):
        rows = pl.ds(b * GROUP, GROUP)
        return jnp.concatenate(
            [
                in_ref[rows, img_at : img_at + img].reshape(img_block, head),
                in_ref[rows, txt_at : txt_at + txt].reshape(txt_block, head),
            ],
            axis=0,
        )

    def store(b, img_at, txt_at, values):
        rows = pl.ds(b * GROUP, GROUP)
        out_ref[rows, img_at : img_at + img] = values[:img_block].reshape(GROUP, img, head)
        out_ref[rows, txt_at : txt_at + txt] = values[img_block:].reshape(GROUP, txt, head)

    def gain_rows(which):
        is_img = lax.broadcasted_iota(jnp.int32, (block, head), 0) < img_block
        return jnp.where(is_img, gains_ref[which : which + 1], gains_ref[which + 2 : which + 3])

    def live_rows(b):
        row = lax.broadcasted_iota(jnp.int32, (block, head), 0)
        return jnp.logical_or(row < img_block, row - img_block + b * txt_block < length)

    def add_terms(which, terms):
        terms_ref[which : which + 1] += jnp.sum(terms[:img_block], axis=0, keepdims=True)
        terms_ref[which + 2 : which + 3] += jnp.sum(terms[img_block:], axis=0, keepdims=True)

    if not values_part:
        acc_ref[...] = jnp.zeros_like(acc_ref)
        terms_ref[...] = jnp.zeros_like(terms_ref)

    for b in range(blocks):
        at = slice(b * block, (b + 1) * block)
        live = live_rows(b)
        raw = load(b, img, in_txt + txt).astype(F32)
        normed = raw * inverse_rms(raw) * gain_rows(1)
        kn_ref[at, :] = jnp.where(live, normed, 0.0).astype(BF16)
        values = load(b, 2 * img, in_txt + 2 * txt).astype(F32)
        vaug_ref[at, :head] = jnp.where(live, values, 0.0).astype(BF16)
        vaug_ref[at, head:] = jnp.where(live, 1.0, 0.0).astype(BF16)

    by_rows = (((1,), (1,)), ((), ()))

    def forward(b, held):
        raw = load(b, 0, in_txt).astype(F32)
        gain = gain_rows(0)
        qn = (raw * inverse_rms(raw) * gain).astype(BF16)
        summed = jnp.zeros((block, 2 * head), F32)
        for start in range(0, full, tile):
            keys = slice(start, start + tile)
            scores = lax.dot_general(qn, kn_ref[keys, :], by_rows, preferred_element_type=F32)
            expo = jnp.exp2(scores * to_exp2).astype(BF16)
            held[:, keys] = expo
            summed += jnp.dot(expo, vaug_ref[keys, :], preferred_element_type=F32)
        per_total = 1.0 / summed[:, head:]
        return raw, gain, qn, summed[:, :head] * per_total, per_total

    def values_backward(b, held, raw, gain, qn, out, per_total):
        store(b, 0, img, out.astype(BF16))
        cot32 = load(b, in_cot, in_cot + img).astype(F32)
        cot_t = jnp.transpose((cot32 * per_total).astype(BF16))
        for start in range(0, full, tile):
            keys = slice(start, start + tile)
            sums = jnp.dot(cot_t, held[:, keys], preferred_element_type=F32)
            acc_ref[:, keys] = sums if b == 0 else acc_ref[:, keys] + sums

    def scores_backward(b, held, raw, gain, qn, out, per_total):
        cot = load(b, in_cot, in_cot + img)
        delta = jnp.sum(out * cot.astype(F32), axis=-1, keepdims=True)
        qn_t = jnp.transpose((qn.astype(F32) * (per_total * scale)).astype(BF16))
        dq = jnp.zeros((block, head), F32)
        for start in range(0, full, tile):
            keys = slice(start, start + tile)
            dprobs = lax.dot_general(
                cot, vaug_ref[keys, :head], by_rows, preferred_element_type=F32
            )
            dscores = held[:, keys] * (dprobs - delta).astype(BF16)
            dq += jnp.dot(dscores, kn_ref[keys, :], preferred_element_type=F32)
            acc_ref[:, keys] += jnp.dot(qn_t, dscores, preferred_element_type=F32)
        grad, terms = norm_backward(raw, gain, dq * (per_total * scale))
        store(b, 0, out_txt, grad.astype(BF16))
        add_terms(0, terms)

    if values_part:
        held = [eb_ref.at[b] for b in range(blocks)]
        results = [forward(0, held[0])]
        for b in range(blocks):
            if b + 1 < blocks:
                results.append(forward(b + 1, held[b + 1]))
            values_backward(b, held[b], *results[b])
        for b in range(blocks):
            at = slice(b * block, (b + 1) * block)
            col = lax.broadcasted_iota(jnp.int32, (head, block), 1)
            live = jnp.logical_or(col < img_block, col - img_block + b * txt_block < length)
            dv_t = jnp.where(live, acc_ref[:, at], 0.0).astype(BF16)
            store(b, out_dv, out_dv + img, jnp.transpose(dv_t))
        return

    @pl.loop(0, blocks, step=2)
    def _queries(b):
        first = forward(b, eb_ref.at[0])
        second = forward(b + 1, eb_ref.at[1])
        scores_backward(b, eb_ref.at[0], *first)
        scores_backward(b + 1, eb_ref.at[1], *second)

    @pl.loop(0, blocks)
    def _key_grads(b):
        at = pl.ds(pl.multiple_of(b * block, block), block)
        upstream = jnp.where(live_rows(b), jnp.transpose(acc_ref[:, at]), 0.0)
        raw = load(b, img, in_txt + txt).astype(F32)
        grad, terms = norm_backward(raw, gain_rows(1), upstream)
        store(b, img, out_txt + txt, grad.astype(BF16))
        add_terms(1, terms)


def attend_pair(arrived, length, gains, img, txt, values_part, spare_rows):
    devices, _, head = arrived.shape
    rows = 2 * (img + txt) + spare_rows
    full = devices * (img + txt)
    block = GROUP * (img + txt)
    in_vmem = pl.BlockSpec(memory_space=pltpu.VMEM)
    out_shape = [jax.ShapeDtypeStruct((devices, rows, head), BF16)]
    if not values_part:
        out_shape.append(jax.ShapeDtypeStruct((4, head), F32))
    return pl.pallas_call(
        functools.partial(pair_kernel, img, txt, values_part),
        out_shape=out_shape,
        in_specs=[pl.BlockSpec(memory_space=pltpu.SMEM), in_vmem, in_vmem],
        out_specs=[in_vmem] * len(out_shape),
        scratch_shapes=[
            pltpu.VMEM((full, head), BF16),
            pltpu.VMEM((full, 2 * head), BF16),
            pltpu.VMEM((full // block if values_part else 2, block, full), BF16),
            pltpu.VMEM((head, full), F32),
        ],
        compiler_params=pltpu.CompilerParams(vmem_limit_bytes=(57 if values_part else 40) * 1024 * 1024),
        cost_estimate=pl.CostEstimate(
            flops=(6 if values_part else 10) * full * full * head,
            bytes_accessed=4 * devices * rows * head,
            transcendentals=full * full,
        ),
        name="attend_values" if values_part else "attend_scores",
    )(length, gains, arrived)


def pack_kernel(*refs):
    *parts, out_ref, held, in_sems, out_sems = refs
    step = held.shape[0] // PACK_CHUNKS
    arriving = []
    for c in range(PACK_CHUNKS):
        pairs = slice(c * step, (c + 1) * step)
        chunk = []
        at = 0
        for i, part in enumerate(parts):
            rows = slice(at, at + part.shape[1])
            copy = pltpu.make_async_copy(part.at[pairs], held.at[pairs, rows], in_sems.at[c, i])
            copy.start()
            chunk.append(copy)
            at += part.shape[1]
        arriving.append(chunk)
    leaving = []
    for c in range(PACK_CHUNKS):
        pairs = slice(c * step, (c + 1) * step)
        for copy in arriving[c]:
            copy.wait()
        copy = pltpu.make_async_copy(held.at[pairs], out_ref.at[pairs], out_sems.at[c])
        copy.start()
        leaving.append(copy)
    for copy in leaving:
        copy.wait()


def pack_rows(*parts):
    pairs, _, head = parts[0].shape
    rows = sum(part.shape[1] for part in parts)
    return pl.pallas_call(
        pack_kernel,
        out_shape=jax.ShapeDtypeStruct((pairs, rows, head), BF16),
        in_specs=[pl.BlockSpec(memory_space=pl.ANY)] * len(parts),
        out_specs=pl.BlockSpec(memory_space=pl.ANY),
        scratch_shapes=[
            pltpu.VMEM((pairs, rows, head), BF16),
            pltpu.SemaphoreType.DMA((PACK_CHUNKS, len(parts))),
            pltpu.SemaphoreType.DMA((PACK_CHUNKS,)),
        ],
        name="pack_rows",
    )(*parts)


def join_kernel(img, txt, values_ref, scores_ref, img_ref, txt_ref, sems):
    own = img + txt
    copies = [
        pltpu.make_async_copy(source, target, sems.at[i])
        for i, (source, target) in enumerate(
            [
                (scores_ref.at[:, : 2 * img], img_ref.at[:, : 2 * img]),
                (values_ref.at[:, own : own + img], img_ref.at[:, 2 * img :]),
                (scores_ref.at[:, 2 * img : 2 * own], txt_ref.at[:, : 2 * txt]),
                (values_ref.at[:, own + img :], txt_ref.at[:, 2 * txt :]),
            ]
        )
    ]
    for copy in copies:
        copy.start()
    for copy in copies:
        copy.wait()


def join_grads(values, scores, img, txt):
    pairs, _, head = values.shape
    return pl.pallas_call(
        functools.partial(join_kernel, img, txt),
        out_shape=[
            jax.ShapeDtypeStruct((pairs, 3 * img, head), BF16),
            jax.ShapeDtypeStruct((pairs, 3 * txt, head), BF16),
        ],
        in_specs=[pl.BlockSpec(memory_space=pltpu.VMEM)] * 2,
        out_specs=[pl.BlockSpec(memory_space=pl.ANY)] * 2,
        scratch_shapes=[pltpu.SemaphoreType.DMA((4,))],
        compiler_params=pltpu.CompilerParams(vmem_limit_bytes=16 * 1024 * 1024),
        name="join_grads",
    )(values, scores)


def split_rows(term):
    high = lax.reduce_precision(term, 8, 7)
    return jnp.concatenate([high, term - high], axis=0).astype(BF16)


def sum_pairwise(term, axis, steps):
    count = lax.axis_size(axis)
    for step in steps:
        term = term + lax.ppermute(term, axis, [(i, i ^ step) for i in range(count)])
    return term


def powers_of_two(count):
    return [1 << bit for bit in range(count.bit_length() - 1)]


def per_device(img_qkv, txt_qkv, img_cot, txt_cot, lengths, norm_gains):
    samples, heads, _, img, head = img_qkv.shape
    txt = txt_qkv.shape[3]
    pairs = samples * heads
    devices = lax.axis_size("seq")
    assert pairs == devices
    outgoing = pack_rows(
        img_qkv.reshape(pairs, 3 * img, head),
        txt_qkv.reshape(pairs, 3 * txt, head),
        img_cot.reshape(pairs, img, head),
        txt_cot.reshape(pairs, txt, head),
    )
    arrived = lax.all_to_all(outgoing, "seq", split_axis=0, concat_axis=0, tiled=True)
    sample = lax.axis_index("seq") // heads
    length = lax.dynamic_slice_in_dim(lengths, sample, 1, 0)
    (values_out,) = attend_pair(arrived, length, norm_gains, img, txt, True, 0)
    values_out, arrived = lax.optimization_barrier((values_out, arrived))
    values_back = lax.all_to_all(values_out, "seq", split_axis=0, concat_axis=0, tiled=True)
    scores_out, terms = attend_pair(arrived, length, norm_gains, img, txt, False, SPARE_ROWS)
    for axis in ("grp", "dp"):
        terms = sum_pairwise(terms, axis, powers_of_two(lax.axis_size(axis)))
    own = img + txt
    split = split_rows(terms)
    scores_out = lax.dynamic_update_slice(
        scores_out, jnp.broadcast_to(split[None], (devices,) + split.shape), (0, 2 * own, 0)
    )
    scores_back = lax.all_to_all(scores_out, "seq", split_axis=0, concat_axis=0, tiled=True)
    group_terms = jnp.sum(scores_back[:, 2 * own :].astype(F32), axis=0)
    gain_grad = group_terms[:4] + group_terms[4:]

    def in_samples(rows):
        return rows.reshape(samples, heads, -1, rows.shape[1], head)

    img_out = in_samples(values_back[:, :img])[:, :, 0]
    txt_out = in_samples(values_back[:, img:own])[:, :, 0]
    img_grad, txt_grad = join_grads(values_back, scores_back, img, txt)
    img_grad = img_grad.reshape(samples, heads, 3, img, head)
    txt_grad = txt_grad.reshape(samples, heads, 3, txt, head)
    return (img_out, txt_out, img_grad, txt_grad, gain_grad)


def solution(mesh):
    rows = P(("grp", "dp"), None, "seq", None)
    grads = P(("grp", "dp"), None, None, "seq", None)
    return jax.shard_map(
        per_device,
        mesh=mesh,
        in_specs=(grads, grads, rows, rows, P(("grp", "dp")), P()),
        out_specs=(rows, rows, grads, grads, P()),
        check_vma=False,
    )
```
